256 devices in a mesh: row: 16 (over z, x_lo), col: 16 (over y, x_hi, core).
Axes of the slice: x: 4 (x_hi: 2, x_lo: 2; x = x_hi * 2 + x_lo), y: 4, z: 8, core: 2. Of those that a mesh axis runs over, the one named last changes fastest.
Arguments:
- density: float32 [10240, 10240], P('row', 'col'), may hold values from -6 to 6
- core_hamiltonian: float32 [10240, 10240], P('row', 'col'), may hold values from -6 to 6
- class_tables: float32 [4, 256, 256], replicated, may hold values from -0.375 to 0.375
- shell_scale: float32 [10240], replicated, may hold values from 0.5 to 1.5
- block_place: int32 [640], replicated, may hold values from 0 to 639, as said below
- work_blocks: int32 [256, 32], P(('row', 'col')), may hold values from 0 to 639, as said below
- quartet_bra: int32 [256, 512], P(('row', 'col')), may hold values from 0 to 1023
- quartet_ket: int32 [256, 512], P(('row', 'col')), may hold values from 0 to 1023
- quartet_class: int32 [256, 512], P(('row', 'col')), may hold values from 0 to 3
- quartet_factor: float32 [256, 512], P(('row', 'col')), may hold values from 0.25 to 1
- quartet_count: int32 [256], P(('row', 'col')), may hold values from 1 to 512, 40960 in all
Outputs:
- fock_matrix: float32 [10240, 10240], P('row', 'col')
The draws below stay inside these ranges and needn't reach their ends.
Inputs may be any that keep to these rules, and one draw needn't show every extreme that they name: `block_place`: a permutation of the 640 shell blocks. `work_blocks`: each device's 32 shell blocks are distinct and listed in increasing block_place; exactly 2 of them have places in each run of 40 = 40 consecutive places from 0 (one block row of devices), and likewise exactly 2 in each run of 40 = 40 (one block column of devices).
All inputs are finite; a program needn't handle non-finite values. No bound on the sum of `quartet_count` on one device may be relied on, other than what follows from the above.
Results may differ from the reference program's by a relative error of at most 0.0003.
Values sent between devices are 32-bit elements; how exact they have to be, the bound alone decides.
No kernel may reach another device: no remote copies, remote signals or barrier semaphores. Data moves between devices by JAX's collectives and lax.ppermute only.
A program may use at most 192 MiB of HBM per device.

```python
import math
import jax
import jax.numpy as jnp
import numpy as np
from jax import lax

SHELL = 16
PAIRS = 256
NBF = 10240
NFB = 640
ROW_SHELLS = 40
COL_SHELLS = 40
WORK = 32
CLASSES = 4
QMAX = 512
QAVG = 160
DEVICES = 256


def place_order(key):
    return jax.random.permutation(jax.random.fold_in(key, 91), NFB).astype(jnp.int32)


def draw_block_place(key, part):
    return place_order(key)


def draw_work_blocks(key, part):
    places = place_order(key)
    key = jax.random.fold_in(key, 3)
    stripe = min(ROW_SHELLS, COL_SHELLS)
    stripes = NFB // stripe
    chosen = WORK // stripes
    scores = jax.random.randint(key, (DEVICES, stripes, stripe), 0, 2 ** 30)
    ranked = jnp.sort(jnp.argsort(scores, axis=-1)[..., :chosen], axis=-1)
    positions = ranked + stripe * jnp.arange(stripes)[None, :, None]
    inverse = jnp.argsort(places)
    return inverse[positions.reshape(DEVICES, WORK)].astype(jnp.int32)


def with_ends(drawn, own_key, low, high):
    shape = drawn.shape
    place = [jax.random.randint(jax.random.fold_in(own_key, axis), (), 0, shape[axis]) for axis in range(len(shape))]
    drawn = drawn.at[tuple(place)].set(low)
    longest = shape.index(max(shape))
    place[longest] = (place[longest] + 1) % shape[longest]
    return drawn.at[tuple(place)].set(high)


def steps_of(key, dims, shards, least, largest):
    level, own = 1.0, jax.random.fold_in(key, 6)
    for dim, blocks in shards:
        draws = jnp.exp(jax.random.uniform(jax.random.fold_in(own, dim), (blocks,), jnp.float32, least / len(shards), largest / len(shards)))
        level = level * jnp.repeat(draws, dims[dim] // blocks).reshape([-1 if axis == dim else 1 for axis in range(len(dims))])
    return level


def length_profile(count, total, most, skew):
    loads = [(1 << 20) // math.isqrt(standing ** skew) + 1 for standing in range(2, count + 1)]
    surplus, counts = total - most - (count - 1), [1] * (count - 1)
    while surplus > 0:
        candidates = [i for i in range(count - 1) if counts[i] < most]
        whole, budget = sum([loads[i] for i in candidates]), surplus
        for i in candidates:
            addition = min(most - counts[i], max(1, budget * loads[i] // whole), surplus)
            counts[i] = counts[i] + addition
            surplus = surplus - addition
    return np.array([most] + counts)


def uneven_parts(key, number_of, total, most, slope):
    if number_of == 2:
        one = jax.random.randint(key, (), max(1, total - most), min(most, total - 1) + 1)
        return jnp.stack([one, total - one])
    lengths = jnp.asarray(length_profile(number_of, total, most, slope), jnp.int32)
    twos = (number_of - 1) // 2
    giver, taker = lengths[1:1 + 2 * twos:2], lengths[2:2 + 2 * twos:2]
    room = jnp.minimum(giver - 1, most - taker)
    shifted = jax.random.randint(jax.random.fold_in(key, 1), (twos,), 0, 1 << 20) % (room + 1)
    lengths = lengths.at[1:1 + 2 * twos:2].set(giver - shifted).at[2:2 + 2 * twos:2].set(taker + shifted)
    return lengths[jax.random.permutation(jax.random.fold_in(key, 2), number_of)]


def noise(key, dims, deviation, most, shards=(), dtype=jnp.bfloat16):
    loudness = steps_of(key, dims, shards, -0.22, 0.18) if shards else 1.0
    values = jax.random.normal(key, dims, jnp.float32) * deviation * loudness
    return jnp.minimum(jnp.maximum(values, -most), most).astype(dtype)


def setup_inputs(seed: int = 0) -> dict:
    splits = jax.random.split(jax.random.key(seed), 12)
    density = noise(splits[0], (NBF, NBF), 1.0, 6.0, ((0, 16), (1, 16)), jnp.float32)
    core_hamiltonian = noise(splits[1], (NBF, NBF), 1.0, 6.0, ((0, 16), (1, 16)), jnp.float32)
    class_tables = noise(splits[2], (CLASSES, PAIRS, PAIRS), PAIRS ** -0.5, 0.375, (), jnp.float32)
    shell_scale = jnp.clip(jnp.exp(jax.random.uniform(splits[3], (NBF,), jnp.float32, math.log(0.5), math.log(1.5))), 0.5, 1.5)
    block_place = draw_block_place(jax.random.fold_in(splits[11], 71), 0)
    work_blocks = draw_work_blocks(jax.random.fold_in(splits[11], 71), 0)
    quartet_bra = with_ends(jax.random.randint(splits[6], (DEVICES, QMAX), 0, WORK * WORK), jax.random.fold_in(splits[6], 1), 0, (WORK * WORK) - 1).astype(jnp.int32)
    quartet_ket = with_ends(jax.random.randint(splits[7], (DEVICES, QMAX), 0, WORK * WORK), jax.random.fold_in(splits[7], 1), 0, (WORK * WORK) - 1).astype(jnp.int32)
    quartet_class = with_ends(jax.random.randint(splits[8], (DEVICES, QMAX), 0, CLASSES), jax.random.fold_in(splits[8], 1), 0, CLASSES - 1).astype(jnp.int32)
    quartet_factor = jnp.clip(jnp.exp(math.log(1.0) - 1.3862944 * jax.random.uniform(splits[9], (DEVICES, QMAX), jnp.float32) ** steps_of(splits[9], (DEVICES, QMAX), ((0, 256),), -0.2, 0.2)), 0.25, 1.0)
    quartet_count = uneven_parts(splits[10], DEVICES, QAVG * DEVICES, QMAX, 2).astype(jnp.int32)
    return {"density": density, "core_hamiltonian": core_hamiltonian, "class_tables": class_tables, "shell_scale": shell_scale, "block_place": block_place, "work_blocks": work_blocks, "quartet_bra": quartet_bra, "quartet_ket": quartet_ket, "quartet_class": quartet_class, "quartet_factor": quartet_factor, "quartet_count": quartet_count}


ORDERS = ((3, 4, 0, 1, 2), (1, 2, 0, 3, 4), (2, 4, 0, 1, 3), (1, 3, 0, 2, 4), (2, 3, 0, 1, 4), (1, 4, 0, 2, 3))
COEFFS = (1.0, 1.0, -0.5, -0.5, -0.5, -0.5)


def make_stacks(class_tables):
    classes = class_tables.shape[0]
    pair_width = class_tables.shape[1]
    tensor = class_tables.reshape(classes, SHELL, SHELL, SHELL, SHELL)
    return [jnp.transpose(tensor, layout).reshape(pair_width, classes * pair_width) for layout in ORDERS]


def pair_weights(weights):
    block_count = weights.shape[0]
    shell_width = weights.shape[1]
    outer = weights[:, None, :, None] * weights[None, :, None, :]
    return outer.reshape(block_count * block_count, shell_width * shell_width)


def quartet_terms(scaled, bra_pairs, ket_pairs, klasses, factors, stacks, task_count):
    shell_a = bra_pairs // task_count
    shell_b = bra_pairs % task_count
    shell_c = ket_pairs // task_count
    shell_d = ket_pairs % task_count
    sources = (shell_c * task_count + shell_d, shell_a * task_count + shell_b,
               shell_b * task_count + shell_d, shell_a * task_count + shell_c,
               shell_b * task_count + shell_c, shell_a * task_count + shell_d)
    targets = (sources[1], sources[0], sources[3], sources[2], sources[5], sources[4])
    pair_width = scaled.shape[1]
    classes = stacks[0].shape[1] // pair_width
    select = (klasses[:, None] == jnp.arange(classes)[None, :]).astype(jnp.float32)
    values = []
    for source, table_stack, weighting in zip(sources, stacks, COEFFS):
        product = jnp.dot(scaled[source], table_stack, precision=lax.Precision.HIGHEST)
        product = product.reshape(source.shape[0], classes, pair_width)
        chosen = jnp.sum(product * select[:, :, None], axis=1)
        values.append(chosen * (weighting * factors)[:, None])
    return jnp.concatenate(targets), jnp.concatenate(values)


def reference(density, core_hamiltonian, class_tables, shell_scale, block_place, work_blocks, quartet_bra, quartet_ket, quartet_class, quartet_factor, quartet_count):
    stacks = make_stacks(class_tables)
    density_view = density.reshape(NFB, SHELL, NFB, SHELL)
    scales = shell_scale.reshape(NFB, SHELL)
    slot_index = jnp.arange(QMAX)

    def device_step(totals, items):
        task_list, bra_pairs, ket_pairs, klasses, factors, live_count = items
        places = block_place[task_list]
        blocks = density_view[places[:, None], :, places[None, :], :].reshape(WORK * WORK, PAIRS)
        weights = pair_weights(scales[task_list])
        scaled = blocks * weights
        factors = jnp.where(slot_index < live_count, factors, 0.0)
        targets, values = quartet_terms(scaled, bra_pairs, ket_pairs, klasses, factors, stacks, WORK)
        partial_value = jnp.zeros((WORK * WORK, PAIRS), jnp.float32).at[targets].add(values)
        partial_value = (partial_value * weights).reshape(WORK, WORK, SHELL, SHELL)
        totals = totals.at[places[:, None], :, places[None, :], :].add(partial_value)
        return totals, None

    totals = jnp.zeros((NFB, SHELL, NFB, SHELL), jnp.float32)
    totals = lax.scan(device_step, totals, (work_blocks, quartet_bra, quartet_ket, quartet_class, quartet_factor, quartet_count))[0]
    return core_hamiltonian + totals.reshape(NBF, NBF)
```

```python
import functools

import jax
import jax.numpy as jnp
from jax import lax
from jax.experimental import pallas as pl
from jax.experimental.pallas import tpu as pltpu
from jax.sharding import PartitionSpec as P

SHELL = 16
LANES = 128
SUBLANES = 8
GROUPS = LANES // SHELL
AXES = ("row", "col")
NT = (((1,), (1,)), ((), ()))
NN = (((1,), (0,)), ((), ()))
TN = (((0,), (0,)), ((), ()))


def swap_groups(tile):
    sublane = lax.broadcasted_iota(jnp.int32, tile.shape, 0)
    group = lax.broadcasted_iota(jnp.int32, tile.shape, 1) // SHELL
    for bit in (1, 2, 4):
        low = (sublane & bit) == 0
        left = (group & bit) == 0
        down = pltpu.roll(pltpu.roll(tile, bit, 0), LANES - SHELL * bit, 1)
        if 2 * bit == SUBLANES:
            tile = jnp.where(low == left, tile, down)
        else:
            up = pltpu.roll(pltpu.roll(tile, SUBLANES - bit, 0), SHELL * bit, 1)
            tile = jnp.where(low == left, tile, jnp.where(low, up, down))
    return tile


def split(values):
    high = values.astype(jnp.bfloat16)
    low = (values - high.astype(jnp.float32)).astype(jnp.bfloat16)
    return high, low


def dot(left, right, dims):
    return lax.dot_general(left, right, dims, preferred_element_type=jnp.float32)


def pick_kernel(wanted_ref, density_ref, out_ref, flat_ref):
    row_blocks = density_ref.shape[0] // SHELL
    col_blocks = density_ref.shape[1] // SHELL
    devices = out_ref.shape[0] // SUBLANES

    def flatten(block, carry):
        for half in range(2):
            start = pl.multiple_of(block * SHELL + half * SUBLANES, SUBLANES)
            for tile in range(col_blocks // GROUPS):
                lanes = slice(tile * LANES, (tile + 1) * LANES)
                values = density_ref[pl.ds(start, SUBLANES), lanes]
                place = (block * col_blocks + tile * GROUPS) * 2 + half
                flat_ref[pl.ds(place, SUBLANES, stride=2), :] = swap_groups(values)
        return carry

    lax.fori_loop(0, row_blocks, flatten, 0)

    def pick(device, carry):
        for part in range(4):
            block = wanted_ref[4 * device + part // 2] * col_blocks + wanted_ref[4 * device + 2 + part % 2]
            source = pl.multiple_of(2 * block, 2)
            target = pl.multiple_of(SUBLANES * device + 2 * part, 2)
            out_ref[pl.ds(target, 2), :] = flat_ref[pl.ds(source, 2), :]
        return carry

    lax.fori_loop(0, devices, pick, 0, unroll=4)


def pick_blocks(wanted, density, devices):
    blocks = (density.shape[0] // SHELL) * (density.shape[1] // SHELL)
    return pl.pallas_call(
        pick_kernel,
        out_shape=jax.ShapeDtypeStruct((devices * SUBLANES, LANES), jnp.float32),
        in_specs=[
            pl.BlockSpec(memory_space=pltpu.SMEM),
            pl.BlockSpec(memory_space=pltpu.VMEM),
        ],
        out_specs=pl.BlockSpec(memory_space=pltpu.VMEM),
        scratch_shapes=[pltpu.VMEM((2 * blocks, LANES), jnp.float32)],
        compiler_params=pltpu.CompilerParams(vmem_limit_bytes=40 << 20),
        name="pick_blocks",
    )(wanted, density)


def merge_kernel(wanted_ref, parts_ref, core_ref, out_ref, flat_ref):
    row_blocks = core_ref.shape[0] // SHELL
    col_blocks = core_ref.shape[1] // SHELL
    devices = parts_ref.shape[0] // SUBLANES
    flat_ref[...] = jnp.zeros_like(flat_ref)

    def add(device, carry):
        places = []
        sums = []
        for part in range(4):
            block = wanted_ref[4 * device + part // 2] * col_blocks + wanted_ref[4 * device + 2 + part % 2]
            place = pl.ds(pl.multiple_of(2 * block, 2), 2)
            source = pl.multiple_of(SUBLANES * device + 2 * part, 2)
            places.append(place)
            sums.append(flat_ref[place, :] + parts_ref[pl.ds(source, 2), :])
        for place, value in zip(places, sums):
            flat_ref[place, :] = value
        return carry

    lax.fori_loop(0, devices, add, 0, unroll=4)

    def unflatten(block, carry):
        for half in range(2):
            start = pl.multiple_of(block * SHELL + half * SUBLANES, SUBLANES)
            for tile in range(col_blocks // GROUPS):
                lanes = slice(tile * LANES, (tile + 1) * LANES)
                place = (block * col_blocks + tile * GROUPS) * 2 + half
                values = swap_groups(flat_ref[pl.ds(place, SUBLANES, stride=2), :])
                out_ref[pl.ds(start, SUBLANES), lanes] = core_ref[pl.ds(start, SUBLANES), lanes] + values
        return carry

    lax.fori_loop(0, row_blocks, unflatten, 0)


def merge_blocks(wanted, parts, core):
    blocks = (core.shape[0] // SHELL) * (core.shape[1] // SHELL)
    return pl.pallas_call(
        merge_kernel,
        out_shape=jax.ShapeDtypeStruct(core.shape, jnp.float32),
        in_specs=[
            pl.BlockSpec(memory_space=pltpu.SMEM),
            pl.BlockSpec(memory_space=pltpu.VMEM),
            pl.BlockSpec(memory_space=pltpu.VMEM),
        ],
        out_specs=pl.BlockSpec(memory_space=pltpu.VMEM),
        scratch_shapes=[pltpu.VMEM((2 * blocks, LANES), jnp.float32)],
        compiler_params=pltpu.CompilerParams(vmem_limit_bytes=40 << 20),
        name="merge_blocks",
    )(wanted, parts, core)


def table_kernel(tables_ref, out_ref, mid_ref, turned_ref, last_ref):
    table = tables_ref[0]
    width = table.shape[0]
    halves = range(2)
    high, low = split(table)
    out_ref[0, 0, 0] = high
    out_ref[0, 0, 1] = low

    def swap_inner(first, carry):
        for a in halves:
            for b in halves:
                rows = pl.ds(pl.multiple_of(first * SHELL + SUBLANES * a, SUBLANES), SUBLANES)
                values = tables_ref[0, rows, LANES * b:LANES * (b + 1)]
                rows = pl.ds(pl.multiple_of(first * SHELL + SUBLANES * b, SUBLANES), SUBLANES)
                mid_ref[rows, LANES * a:LANES * (a + 1)] = swap_groups(values)
        return carry

    lax.fori_loop(0, width // SHELL, swap_inner, 0)
    high, low = split(mid_ref[...])
    out_ref[0, 1, 0] = high
    out_ref[0, 1, 1] = low
    turned = mid_ref[...].T
    for b in halves:
        turned_ref[b] = turned[:, LANES * b:LANES * (b + 1)]

    def swap_outer(last, carry):
        for a in halves:
            for b in halves:
                rows = pl.ds(LANES * a + last, SUBLANES, stride=SHELL)
                values = turned_ref[b, rows, :]
                rows = pl.ds(LANES * b + last, SUBLANES, stride=SHELL)
                last_ref[a, rows, :] = swap_groups(values)
        return carry

    lax.fori_loop(0, SHELL, swap_outer, 0)
    for a in halves:
        high, low = split(last_ref[a])
        out_ref[0, 2, 0, :, LANES * a:LANES * (a + 1)] = high
        out_ref[0, 2, 1, :, LANES * a:LANES * (a + 1)] = low


def make_tables(class_tables):
    classes, width, _ = class_tables.shape
    return pl.pallas_call(
        table_kernel,
        grid=(classes,),
        out_shape=jax.ShapeDtypeStruct((classes, 3, 2, width, width), jnp.bfloat16),
        in_specs=[pl.BlockSpec((1, width, width), lambda c: (c, 0, 0))],
        out_specs=pl.BlockSpec((1, 3, 2, width, width), lambda c: (c, 0, 0, 0, 0)),
        scratch_shapes=[
            pltpu.VMEM((width, width), jnp.float32),
            pltpu.VMEM((2, width, LANES), jnp.float32),
            pltpu.VMEM((2, width, LANES), jnp.float32),
        ],
        compiler_params=pltpu.CompilerParams(vmem_limit_bytes=40 << 20),
        name="make_tables",
    )(class_tables)


def quartet_kernel(
    count_ref, blocks_ref, left_ref, right_ref, columns_ref, rows_ref, weights_ref, tables_ref,
    out_ref, scaled_ref, pieces_ref, totals_ref,
):
    slots, classes = weights_ref.shape
    pairs = pieces_ref.shape[0]
    width = totals_ref.shape[1]
    step_rows = 128
    scaled_ref[...] = (blocks_ref[...].reshape(16, 16, SUBLANES, LANES) * left_ref[...][:, None]
                       * right_ref[...][None]).reshape(scaled_ref.shape)
    for half in range(2):
        high, low = split(scaled_ref[pl.ds(half, pairs, stride=2), :])
        pieces_ref[:, LANES * half:LANES * (half + 1)] = high
        pieces_ref[:, width + LANES * half:width + LANES * (half + 1)] = low
    totals_ref[...] = jnp.zeros_like(totals_ref)

    def step(index, carry):
        here = pl.ds(pl.multiple_of(index * step_rows, step_rows), step_rows)
        lane = lax.broadcasted_iota(jnp.int32, (step_rows, pairs), 1)
        weights = weights_ref[here, :]
        values_high = []
        values_low = []
        for kind in range(6):
            column = columns_ref[here, kind:kind + 1]
            chosen = jnp.where(lane == column, 1.0, 0.0).astype(jnp.bfloat16)
            found = dot(chosen, pieces_ref[...], NN).astype(jnp.bfloat16)
            high, low = found[:, :width], found[:, width:]
            form = kind // 2
            dims = NT if kind % 2 == 0 else NN
            total = jnp.zeros((step_rows, width), jnp.float32)
            for klass in range(classes):
                product = dot(high, tables_ref[klass, form, 0], dims)
                product += dot(high, tables_ref[klass, form, 1], dims)
                product += dot(low, tables_ref[klass, form, 0], dims)
                total += product * weights[:, klass:klass + 1]
            if kind >= 2:
                total = total * -0.5
            high, low = split(total)
            values_high.append(high)
            values_low.append(low)
        sublane = lax.broadcasted_iota(jnp.int32, (pairs, step_rows), 0)
        sums = totals_ref[...]
        for kind in range(6):
            row = rows_ref[kind ^ 1:(kind ^ 1) + 1, here]
            chosen = jnp.where(sublane == row, 1.0, 0.0).astype(jnp.bfloat16)
            sums += dot(chosen, values_high[kind], NN) + dot(chosen, values_low[kind], NN)
        totals_ref[...] = sums
        return carry

    lax.fori_loop(0, (count_ref[0] + step_rows - 1) // step_rows, step, 0)
    for half in range(2):
        scaled_ref[pl.ds(half, pairs, stride=2), :] = totals_ref[:, LANES * half:LANES * (half + 1)]
    out_ref[...] = (scaled_ref[...].reshape(16, 16, SUBLANES, LANES) * left_ref[...][:, None]
                    * right_ref[...][None]).reshape(out_ref.shape)


def add_quartets(count, blocks, left, right, columns, rows, weights, tables):
    lines = blocks.shape[0]
    width = tables.shape[-1]
    vmem = pl.BlockSpec(memory_space=pltpu.VMEM)
    return pl.pallas_call(
        quartet_kernel,
        out_shape=jax.ShapeDtypeStruct(blocks.shape, jnp.float32),
        in_specs=[pl.BlockSpec(memory_space=pltpu.SMEM)] + [vmem] * 7,
        out_specs=vmem,
        scratch_shapes=[
            pltpu.VMEM((lines, LANES), jnp.float32),
            pltpu.VMEM((lines // 2, 2 * width), jnp.bfloat16),
            pltpu.VMEM((lines // 2, width), jnp.float32),
        ],
        compiler_params=pltpu.CompilerParams(vmem_limit_bytes=56 << 20),
        name="add_quartets",
    )(count, blocks, left, right, columns, rows, weights, tables)


def exchange(values):
    return lax.all_to_all(values, AXES, split_axis=0, concat_axis=0, tiled=True)


def on_device(
    density,
    core_hamiltonian,
    class_tables,
    shell_scale,
    block_place,
    work_blocks,
    quartet_bra,
    quartet_ket,
    quartet_class,
    quartet_factor,
    quartet_count,
):
    row_count = lax.axis_size("row")
    col_count = lax.axis_size("col")
    devices = row_count * col_count
    task_count = work_blocks.shape[1]
    row_blocks = density.shape[0] // SHELL
    col_blocks = density.shape[1] // SHELL
    classes = class_tables.shape[0]
    own_tasks = work_blocks[0]
    places = block_place[own_tasks]
    row_part = (places % row_blocks).reshape(row_count, 2)
    col_part = (places % col_blocks).reshape(col_count, 2)
    outgoing = jnp.concatenate(
        (
            jnp.broadcast_to(row_part[:, None, :], (row_count, col_count, 2)),
            jnp.broadcast_to(col_part[None, :, :], (row_count, col_count, 2)),
        ),
        axis=2,
    )
    wanted = exchange(outgoing.reshape(devices, 4)).reshape(devices * 4)
    picked = pick_blocks(wanted, density, devices)
    blocks = exchange(picked.reshape(devices, SUBLANES, LANES))
    blocks = blocks.reshape(devices * SUBLANES, LANES)

    tables = make_tables(class_tables)
    scales = shell_scale.reshape(-1, SHELL)[own_tasks]
    left = jnp.broadcast_to(
        scales.reshape(row_count, 2, 1, 2, SUBLANES, 1), (row_count, 2, 2, 2, SUBLANES, SHELL)
    ).reshape(row_count, SUBLANES, LANES)
    right = jnp.broadcast_to(
        scales.reshape(col_count, 1, 2, 1, 1, SHELL), (col_count, 2, 2, 2, SUBLANES, SHELL)
    ).reshape(col_count, SUBLANES, LANES)
    bra, ket = quartet_bra[0], quartet_ket[0]
    shell_a, shell_b = bra // task_count, bra % task_count
    shell_c, shell_d = ket // task_count, ket % task_count

    def line(first, second):
        return ((first // 2) * col_count + second // 2) * 4 + (first % 2) * 2 + second % 2

    rows = jnp.stack(
        (
            line(shell_c, shell_d),
            line(shell_a, shell_b),
            line(shell_b, shell_d),
            line(shell_a, shell_c),
            line(shell_b, shell_c),
            line(shell_a, shell_d),
        )
    )
    slots = rows.shape[1]
    live = jnp.where(jnp.arange(slots) < quartet_count[0], quartet_factor[0], 0.0)
    weights = jnp.where(quartet_class[0][:, None] == jnp.arange(classes)[None, :], live[:, None], 0.0)
    summed = add_quartets(quartet_count, blocks, left, right, rows.T, rows, weights, tables)
    returned = exchange(summed.reshape(devices, SUBLANES, LANES))
    return merge_blocks(wanted, returned.reshape(devices * SUBLANES, LANES), core_hamiltonian)


def solution(mesh):
    placed = (
        P("row", "col"),
        P("row", "col"),
        P(),
        P(),
        P(),
        P(("row", "col"), None),
        P(("row", "col"), None),
        P(("row", "col"), None),
        P(("row", "col"), None),
        P(("row", "col"), None),
        P(("row", "col")),
    )
    return jax.shard_map(
        on_device, mesh=mesh, in_specs=placed, out_specs=P("row", "col"), check_vma=False
    )
```

```python
import functools

import jax
import jax.numpy as jnp
from jax import lax
from jax.experimental import pallas as pl
from jax.experimental.pallas import tpu as pltpu
from jax.sharding import PartitionSpec as P

SHELL = 16
LANES = 128
SUBLANES = 8
GROUPS = LANES // SHELL
AXES = ("row", "col")
NT = (((1,), (1,)), ((), ()))
NN = (((1,), (0,)), ((), ()))


def swap_groups(tile):
    sublane = lax.broadcasted_iota(jnp.int32, tile.shape, 0)
    lane = lax.broadcasted_iota(jnp.int32, tile.shape, 1)
    group, inner = lane // SHELL, lane % SHELL
    tile = jnp.take_along_axis(tile, ((sublane + group) % GROUPS) * SHELL + inner, axis=1)
    tile = jnp.take_along_axis(tile, (sublane - group) % SUBLANES, axis=0)
    return jnp.take_along_axis(tile, ((sublane - group) % GROUPS) * SHELL + inner, axis=1)


def split(values):
    high = values.astype(jnp.bfloat16)
    low = (values - high.astype(jnp.float32)).astype(jnp.bfloat16)
    return high, low


def dot(left, right, dims):
    return lax.dot_general(left, right, dims, preferred_element_type=jnp.float32)


def flatten_kernel(density_ref, flat_ref):
    row_blocks = density_ref.shape[0] // SHELL
    col_blocks = density_ref.shape[1] // SHELL

    def flatten(block, carry):
        for half in range(2):
            start = pl.multiple_of(block * SHELL + half * SUBLANES, SUBLANES)
            for tile in range(col_blocks // GROUPS):
                lanes = slice(tile * LANES, (tile + 1) * LANES)
                values = density_ref[pl.ds(start, SUBLANES), lanes]
                place = (block * col_blocks + tile * GROUPS) * 2 + half
                flat_ref[pl.ds(place, SUBLANES, stride=2), :] = swap_groups(values)
        return carry

    lax.fori_loop(0, row_blocks, flatten, 0, unroll=8)


def flatten_blocks(density):
    blocks = (density.shape[0] // SHELL) * (density.shape[1] // SHELL)
    return pl.pallas_call(
        flatten_kernel,
        out_shape=jax.ShapeDtypeStruct((2 * blocks, LANES), jnp.float32),
        name="flatten_blocks",
    )(density)


def pick_kernel(wanted_ref, flat_ref, out_ref):
    def pick(device, carry):
        for part in range(4):
            source = pl.multiple_of(wanted_ref[4 * device + part // 2] + wanted_ref[4 * device + 2 + part % 2], 2)
            target = pl.multiple_of(SUBLANES * device + 2 * part, 2)
            out_ref[pl.ds(target, 2), :] = flat_ref[pl.ds(source, 2), :]
        return carry

    lax.fori_loop(0, out_ref.shape[0] // SUBLANES, pick, 0, unroll=8)


def pick_blocks(wanted, flat, devices):
    return pl.pallas_call(
        pick_kernel,
        out_shape=jax.ShapeDtypeStruct((devices * SUBLANES, LANES), jnp.float32),
        in_specs=[
            pl.BlockSpec(memory_space=pltpu.SMEM),
            pl.BlockSpec(memory_space=pltpu.VMEM),
        ],
        out_specs=pl.BlockSpec(memory_space=pltpu.VMEM),
        name="pick_blocks",
    )(wanted, flat)


def merge_kernel(wanted_ref, parts_ref, core_ref, out_ref, flat_ref):
    row_blocks = core_ref.shape[0] // SHELL
    col_blocks = core_ref.shape[1] // SHELL
    devices = parts_ref.shape[0] // SUBLANES
    flat_ref[...] = jnp.zeros_like(flat_ref)

    def add(device, carry):
        places = []
        sums = []
        for part in range(4):
            place = wanted_ref[4 * device + part // 2] + wanted_ref[4 * device + 2 + part % 2]
            place = pl.ds(pl.multiple_of(place, 2), 2)
            source = pl.multiple_of(SUBLANES * device + 2 * part, 2)
            places.append(place)
            sums.append(flat_ref[place, :] + parts_ref[pl.ds(source, 2), :])
        for place, value in zip(places, sums):
            flat_ref[place, :] = value
        return carry

    lax.fori_loop(0, devices, add, 0, unroll=8)

    def unflatten(block, carry):
        for half in range(2):
            start = pl.multiple_of(block * SHELL + half * SUBLANES, SUBLANES)
            for tile in range(col_blocks // GROUPS):
                lanes = slice(tile * LANES, (tile + 1) * LANES)
                place = (block * col_blocks + tile * GROUPS) * 2 + half
                values = swap_groups(flat_ref[pl.ds(place, SUBLANES, stride=2), :])
                out_ref[pl.ds(start, SUBLANES), lanes] = core_ref[pl.ds(start, SUBLANES), lanes] + values
        return carry

    lax.fori_loop(0, row_blocks, unflatten, 0, unroll=8)


def merge_blocks(wanted, parts, core):
    blocks = (core.shape[0] // SHELL) * (core.shape[1] // SHELL)
    return pl.pallas_call(
        merge_kernel,
        out_shape=jax.ShapeDtypeStruct(core.shape, jnp.float32),
        in_specs=[
            pl.BlockSpec(memory_space=pltpu.SMEM),
            pl.BlockSpec(memory_space=pltpu.VMEM),
            pl.BlockSpec(memory_space=pltpu.VMEM),
        ],
        out_specs=pl.BlockSpec(memory_space=pltpu.VMEM),
        scratch_shapes=[pltpu.VMEM((2 * blocks, LANES), jnp.float32)],
        compiler_params=pltpu.CompilerParams(vmem_limit_bytes=40 << 20),
        name="merge_blocks",
    )(wanted, parts, core)


def table_kernel(tables_ref, out_ref, mid_ref, turned_ref, last_ref):
    table = tables_ref[0]
    width = table.shape[0]
    halves = range(2)
    high, low = split(table)
    out_ref[0, 0, 0] = high
    out_ref[0, 0, 1] = low

    def swap_inner(first, carry):
        for a in halves:
            for b in halves:
                rows = pl.ds(pl.multiple_of(first * SHELL + SUBLANES * a, SUBLANES), SUBLANES)
                values = tables_ref[0, rows, LANES * b:LANES * (b + 1)]
                rows = pl.ds(pl.multiple_of(first * SHELL + SUBLANES * b, SUBLANES), SUBLANES)
                mid_ref[rows, LANES * a:LANES * (a + 1)] = swap_groups(values)
        return carry

    lax.fori_loop(0, width // SHELL, swap_inner, 0, unroll=4)
    high, low = split(mid_ref[...])
    out_ref[0, 1, 0] = high
    out_ref[0, 1, 1] = low
    turned = mid_ref[...].T
    for b in halves:
        turned_ref[b] = turned[:, LANES * b:LANES * (b + 1)]

    def swap_outer(last, carry):
        for a in halves:
            for b in halves:
                rows = pl.ds(LANES * a + last, SUBLANES, stride=SHELL)
                values = turned_ref[b, rows, :]
                rows = pl.ds(LANES * b + last, SUBLANES, stride=SHELL)
                last_ref[a, rows, :] = swap_groups(values)
        return carry

    lax.fori_loop(0, SHELL, swap_outer, 0, unroll=4)
    for a in halves:
        high, low = split(last_ref[a])
        out_ref[0, 2, 0, :, LANES * a:LANES * (a + 1)] = high
        out_ref[0, 2, 1, :, LANES * a:LANES * (a + 1)] = low


def make_tables(class_tables):
    classes, width, _ = class_tables.shape
    return pl.pallas_call(
        table_kernel,
        grid=(classes,),
        out_shape=jax.ShapeDtypeStruct((classes, 3, 2, width, width), jnp.bfloat16),
        in_specs=[pl.BlockSpec((1, width, width), lambda c: (c, 0, 0))],
        out_specs=pl.BlockSpec((1, 3, 2, width, width), lambda c: (c, 0, 0, 0, 0)),
        scratch_shapes=[
            pltpu.VMEM((width, width), jnp.float32),
            pltpu.VMEM((2, width, LANES), jnp.float32),
            pltpu.VMEM((2, width, LANES), jnp.float32),
        ],
        compiler_params=pltpu.CompilerParams(vmem_limit_bytes=40 << 20),
        name="make_tables",
    )(class_tables)


def sort_kernel(count_ref, bra_ref, ket_ref, class_ref, factor_ref, columns_ref, rows_ref):
    slots = bra_ref.shape[1]
    bra, ket = bra_ref[...], ket_ref[...]
    shell_a, shell_b = bra // 32, bra % 32
    shell_c, shell_d = ket // 32, ket % 32
    slot = lax.broadcasted_iota(jnp.int32, (1, slots), 1)
    live = slot < count_ref[0]
    klass = jnp.where(live, class_ref[...], SUBLANES - 1)
    factor = jnp.where(live, factor_ref[...], 0.0)

    def line(first, second):
        return (((first // 2) * 16 + second // 2) * 4 + (first % 2) * 2 + second % 2).astype(jnp.float32)

    fields = jnp.concatenate(
        (
            line(shell_c, shell_d),
            line(shell_a, shell_b),
            line(shell_b, shell_d),
            line(shell_a, shell_c),
            line(shell_b, shell_c),
            line(shell_a, shell_d),
            klass.astype(jnp.float32),
            factor,
        ),
        axis=0,
    )
    number = lax.broadcasted_iota(jnp.int32, (SUBLANES, slots), 0)
    same = jnp.where(klass == number, 1.0, 0.0)
    start = jnp.sum(jnp.where(klass < number, 1.0, 0.0), axis=1, keepdims=True)
    low = lax.broadcasted_iota(jnp.int32, (slots, slots), 0)
    high = lax.broadcasted_iota(jnp.int32, (slots, slots), 1)
    before = jnp.where(low < high, 1.0, 0.0).astype(jnp.bfloat16)
    rank = dot(same.astype(jnp.bfloat16), before, NN) + start
    rank = jnp.sum(rank * same, axis=0, keepdims=True).astype(jnp.int32)
    order = jnp.where(low == rank, 1.0, 0.0)
    rows_ref[...] = lax.dot_general(
        fields, order, NT, precision=lax.Precision.HIGHEST, preferred_element_type=jnp.float32
    )
    columns_ref[...] = lax.dot_general(
        order, fields, NT, precision=lax.Precision.HIGHEST, preferred_element_type=jnp.float32
    )


def sort_quartets(count, bra, ket, klass, factor):
    slots = bra.shape[1]
    vmem = pl.BlockSpec(memory_space=pltpu.VMEM)
    return pl.pallas_call(
        sort_kernel,
        out_shape=(
            jax.ShapeDtypeStruct((slots, SUBLANES), jnp.float32),
            jax.ShapeDtypeStruct((SUBLANES, slots), jnp.float32),
        ),
        in_specs=[pl.BlockSpec(memory_space=pltpu.SMEM)] + [vmem] * 4,
        out_specs=(vmem, vmem),
        name="sort_quartets",
    )(count, bra, ket, klass, factor)


STEP = 128


def quartet_kernel(
    ends_ref, blocks_ref, left_ref, right_ref, columns_ref, rows_ref, tables_ref,
    out_ref, scaled_ref, pieces_ref, totals_ref, found_ref, values_ref,
):
    classes = tables_ref.shape[0]
    pairs = pieces_ref.shape[0]
    width = totals_ref.shape[1]
    scaled_ref[...] = (blocks_ref[...].reshape(16, 16, SUBLANES, LANES) * left_ref[...][:, None]
                       * right_ref[...][None]).reshape(scaled_ref.shape)
    for half in range(2):
        high, low = split(scaled_ref[pl.ds(half, pairs, stride=2), :])
        pieces_ref[:, LANES * half:LANES * (half + 1)] = high
        pieces_ref[:, width + LANES * half:width + LANES * (half + 1)] = low
    totals_ref[...] = jnp.zeros_like(totals_ref)

    def step(index, carry):
        base = pl.multiple_of(index * STEP, STEP)
        here = pl.ds(base, STEP)
        columns = columns_ref[here, :]
        lane = lax.broadcasted_iota(jnp.int32, (STEP, pairs), 1)
        chosen = jnp.concatenate(
            [
                jnp.where(lane == columns[:, kind:kind + 1].astype(jnp.int32), 1.0, 0.0).astype(jnp.bfloat16)
                for kind in range(6)
            ],
            axis=0,
        )
        found_ref[...] = dot(chosen, pieces_ref[...], NN).astype(jnp.bfloat16)
        values_ref[...] = jnp.zeros_like(values_ref)
        for klass in range(classes):
            begin = 0 if klass == 0 else ends_ref[klass - 1]

            @pl.when((begin < base + STEP) & (ends_ref[klass] > base) & (begin < ends_ref[klass]))
            def _():
                factor = jnp.where(columns[:, 6:7] == klass, columns[:, 7:8], 0.0)
                for kind in range(6):
                    part = slice(STEP * kind, STEP * (kind + 1))
                    high, low = found_ref[part, :width], found_ref[part, width:]
                    form = kind // 2
                    dims = NT if kind % 2 == 0 else NN
                    product = dot(high, tables_ref[klass, form, 0], dims)
                    product += dot(high, tables_ref[klass, form, 1], dims)
                    product += dot(low, tables_ref[klass, form, 0], dims)
                    values_ref[part, :] += product * (factor if kind < 2 else -0.5 * factor)

        high, low = split(values_ref[...])
        sublane = lax.broadcasted_iota(jnp.int32, (pairs, STEP), 0)
        chosen = jnp.concatenate(
            [
                jnp.where(sublane == rows_ref[kind ^ 1:(kind ^ 1) + 1, here].astype(jnp.int32), 1.0, 0.0).astype(
                    jnp.bfloat16
                )
                for kind in range(6)
            ],
            axis=1,
        )
        totals_ref[...] += dot(chosen, high, NN) + dot(chosen, low, NN)
        return carry

    lax.fori_loop(0, (ends_ref[classes - 1] + STEP - 1) // STEP, step, 0)
    for half in range(2):
        scaled_ref[pl.ds(half, pairs, stride=2), :] = totals_ref[:, LANES * half:LANES * (half + 1)]
    out_ref[...] = (scaled_ref[...].reshape(16, 16, SUBLANES, LANES) * left_ref[...][:, None]
                    * right_ref[...][None]).reshape(out_ref.shape)


def add_quartets(ends, blocks, left, right, columns, rows, tables):
    lines = blocks.shape[0]
    width = tables.shape[-1]
    vmem = pl.BlockSpec(memory_space=pltpu.VMEM)
    return pl.pallas_call(
        quartet_kernel,
        out_shape=jax.ShapeDtypeStruct(blocks.shape, jnp.float32),
        in_specs=[pl.BlockSpec(memory_space=pltpu.SMEM)] + [vmem] * 6,
        out_specs=vmem,
        scratch_shapes=[
            pltpu.VMEM((lines, LANES), jnp.float32),
            pltpu.VMEM((lines // 2, 2 * width), jnp.bfloat16),
            pltpu.VMEM((lines // 2, width), jnp.float32),
            pltpu.VMEM((6 * STEP, 2 * width), jnp.bfloat16),
            pltpu.VMEM((6 * STEP, width), jnp.float32),
        ],
        compiler_params=pltpu.CompilerParams(vmem_limit_bytes=56 << 20),
        name="add_quartets",
    )(ends, blocks, left, right, columns, rows, tables)


def exchange(values):
    return lax.all_to_all(values, AXES, split_axis=0, concat_axis=0, tiled=True)


def on_device(
    density,
    core_hamiltonian,
    class_tables,
    shell_scale,
    block_place,
    work_blocks,
    quartet_bra,
    quartet_ket,
    quartet_class,
    quartet_factor,
    quartet_count,
):
    row_count = lax.axis_size("row")
    col_count = lax.axis_size("col")
    devices = row_count * col_count
    row_blocks = density.shape[0] // SHELL
    col_blocks = density.shape[1] // SHELL
    classes = class_tables.shape[0]
    own_tasks = work_blocks[0]
    places = block_place[own_tasks]
    row_part = (places % row_blocks * (2 * col_blocks)).reshape(row_count, 2)
    col_part = (places % col_blocks * 2).reshape(col_count, 2)
    outgoing = jnp.concatenate(
        (
            jnp.broadcast_to(row_part[:, None, :], (row_count, col_count, 2)),
            jnp.broadcast_to(col_part[None, :, :], (row_count, col_count, 2)),
        ),
        axis=2,
    )
    wanted = exchange(outgoing.reshape(devices, 4)).reshape(devices * 4)
    picked = pick_blocks(wanted, flatten_blocks(density), devices)
    blocks = exchange(picked.reshape(devices, SUBLANES, LANES))
    blocks = blocks.reshape(devices * SUBLANES, LANES)

    tables = make_tables(class_tables)
    scales = shell_scale.reshape(-1, SHELL)[own_tasks]
    left = jnp.broadcast_to(
        scales.reshape(row_count, 2, 1, 2, SUBLANES, 1), (row_count, 2, 2, 2, SUBLANES, SHELL)
    ).reshape(row_count, SUBLANES, LANES)
    right = jnp.broadcast_to(
        scales.reshape(col_count, 1, 2, 1, 1, SHELL), (col_count, 2, 2, 2, SUBLANES, SHELL)
    ).reshape(col_count, SUBLANES, LANES)
    columns, rows = sort_quartets(quartet_count, quartet_bra, quartet_ket, quartet_class, quartet_factor)
    slots = quartet_class.shape[1]
    within = jnp.where(jnp.arange(slots) < quartet_count[0], quartet_class[0], classes)
    ends = jnp.sum((within[None, :] <= jnp.arange(classes)[:, None]).astype(jnp.int32), axis=1)
    summed = add_quartets(ends, blocks, left, right, columns, rows, tables)
    returned = exchange(summed.reshape(devices, SUBLANES, LANES))
    return merge_blocks(wanted, returned.reshape(devices * SUBLANES, LANES), core_hamiltonian)


def solution(mesh):
    placed = (
        P("row", "col"),
        P("row", "col"),
        P(),
        P(),
        P(),
        P(("row", "col"), None),
        P(("row", "col"), None),
        P(("row", "col"), None),
        P(("row", "col"), None),
        P(("row", "col"), None),
        P(("row", "col")),
    )
    return jax.shard_map(
        on_device, mesh=mesh, in_specs=placed, out_specs=P("row", "col"), check_vma=False
    )
```

```python
import functools

import jax
import jax.numpy as jnp
from jax import lax
from jax.experimental import pallas as pl
from jax.experimental.pallas import tpu as pltpu
from jax.sharding import PartitionSpec as P

SHELL = 16
LANES = 128
SUBLANES = 8
VMEM_BYTES = 16 << 20
GROUPS = LANES // SHELL
AXES = ("row", "col")
NT = (((1,), (1,)), ((), ()))
NN = (((1,), (0,)), ((), ()))


def swap_groups(tile):
    sublane = lax.broadcasted_iota(jnp.int32, tile.shape, 0)
    lane = lax.broadcasted_iota(jnp.int32, tile.shape, 1)
    group, inner = lane // SHELL, lane % SHELL
    tile = jnp.take_along_axis(tile, ((sublane + group) % GROUPS) * SHELL + inner, axis=1)
    tile = jnp.take_along_axis(tile, (sublane - group) % SUBLANES, axis=0)
    return jnp.take_along_axis(tile, ((sublane - group) % GROUPS) * SHELL + inner, axis=1)


def split(values):
    high = values.astype(jnp.bfloat16)
    low = (values - high.astype(jnp.float32)).astype(jnp.bfloat16)
    return high, low


def dot(left, right, dims):
    return lax.dot_general(left, right, dims, preferred_element_type=jnp.float32)


def flatten_kernel(density_ref, flat_ref):
    row_blocks = density_ref.shape[0] // SHELL
    col_blocks = density_ref.shape[1] // SHELL

    def flatten(block, carry):
        for half in range(2):
            start = pl.multiple_of(block * SHELL + half * SUBLANES, SUBLANES)
            for tile in range(col_blocks // GROUPS):
                lanes = slice(tile * LANES, (tile + 1) * LANES)
                values = density_ref[pl.ds(start, SUBLANES), lanes]
                place = (block * col_blocks + tile * GROUPS) * 2 + half
                flat_ref[pl.ds(place, SUBLANES, stride=2), :] = swap_groups(values)
        return carry

    lax.fori_loop(0, row_blocks, flatten, 0, unroll=8)


def flatten_blocks(density):
    blocks = (density.shape[0] // SHELL) * (density.shape[1] // SHELL)
    return pl.pallas_call(
        flatten_kernel,
        out_shape=jax.ShapeDtypeStruct((2 * blocks, LANES), jnp.float32),
        compiler_params=pltpu.CompilerParams(vmem_limit_bytes=VMEM_BYTES),
        name="flatten_blocks",
    )(density)


def pick_kernel(wanted_ref, flat_ref, out_ref):
    def pick(device, carry):
        for part in range(4):
            source = pl.multiple_of(wanted_ref[device, 0, part // 2] + wanted_ref[device, 0, 2 + part % 2], 2)
            target = pl.multiple_of(SUBLANES * device + 2 * part, 2)
            out_ref[pl.ds(target, 2), :] = flat_ref[pl.ds(source, 2), :]
        return carry

    lax.fori_loop(0, out_ref.shape[0] // SUBLANES, pick, 0, unroll=8)


def pick_blocks(wanted, flat, devices):
    return pl.pallas_call(
        pick_kernel,
        out_shape=jax.ShapeDtypeStruct((devices * SUBLANES, LANES), jnp.float32),
        in_specs=[
            pl.BlockSpec(memory_space=pltpu.SMEM),
            pl.BlockSpec(memory_space=pltpu.VMEM),
        ],
        out_specs=pl.BlockSpec(memory_space=pltpu.VMEM),
        compiler_params=pltpu.CompilerParams(vmem_limit_bytes=VMEM_BYTES),
        name="pick_blocks",
    )(wanted, flat)


def merge_kernel(wanted_ref, parts_ref, core_ref, out_ref, flat_ref):
    row_blocks = core_ref.shape[0] // SHELL
    col_blocks = core_ref.shape[1] // SHELL
    devices = parts_ref.shape[0] // SUBLANES
    flat_ref[...] = jnp.zeros_like(flat_ref)

    def add(device, carry):
        places = []
        sums = []
        for part in range(4):
            place = wanted_ref[device, 0, part // 2] + wanted_ref[device, 0, 2 + part % 2]
            place = pl.ds(pl.multiple_of(place, 2), 2)
            source = pl.multiple_of(SUBLANES * device + 2 * part, 2)
            places.append(place)
            sums.append(flat_ref[place, :] + parts_ref[pl.ds(source, 2), :])
        for place, value in zip(places, sums):
            flat_ref[place, :] = value
        return carry

    lax.fori_loop(0, devices, add, 0, unroll=8)

    def unflatten(block, carry):
        for half in range(2):
            start = pl.multiple_of(block * SHELL + half * SUBLANES, SUBLANES)
            for tile in range(col_blocks // GROUPS):
                lanes = slice(tile * LANES, (tile + 1) * LANES)
                place = (block * col_blocks + tile * GROUPS) * 2 + half
                values = swap_groups(flat_ref[pl.ds(place, SUBLANES, stride=2), :])
                out_ref[pl.ds(start, SUBLANES), lanes] = core_ref[pl.ds(start, SUBLANES), lanes] + values
        return carry

    lax.fori_loop(0, row_blocks, unflatten, 0, unroll=8)


def merge_blocks(wanted, parts, core):
    blocks = (core.shape[0] // SHELL) * (core.shape[1] // SHELL)
    return pl.pallas_call(
        merge_kernel,
        out_shape=jax.ShapeDtypeStruct(core.shape, jnp.float32),
        in_specs=[
            pl.BlockSpec(memory_space=pltpu.SMEM),
            pl.BlockSpec(memory_space=pltpu.VMEM),
            pl.BlockSpec(memory_space=pltpu.VMEM),
        ],
        out_specs=pl.BlockSpec(memory_space=pltpu.VMEM),
        scratch_shapes=[pltpu.VMEM((2 * blocks, LANES), jnp.float32)],
        compiler_params=pltpu.CompilerParams(vmem_limit_bytes=VMEM_BYTES),
        name="merge_blocks",
    )(wanted, parts, core)


def table_kernel(tables_ref, out_ref, mid_ref, turned_ref, last_ref):
    width = tables_ref.shape[1]
    halves = range(2)

    def keep(form, values):
        out_ref[0, form, 0], out_ref[0, form, 1] = split(values)

    keep(0, tables_ref[0])

    def swap_inner(first, carry):
        for a in halves:
            for b in halves:
                rows = pl.ds(pl.multiple_of(first * SHELL + SUBLANES * a, SUBLANES), SUBLANES)
                values = tables_ref[0, rows, LANES * b:LANES * (b + 1)]
                rows = pl.ds(pl.multiple_of(first * SHELL + SUBLANES * b, SUBLANES), SUBLANES)
                mid_ref[rows, LANES * a:LANES * (a + 1)] = swap_groups(values)
        return carry

    lax.fori_loop(0, width // SHELL, swap_inner, 0, unroll=4)
    turned = mid_ref[...].T
    keep(1, mid_ref[...])
    for b in halves:
        turned_ref[b] = turned[:, LANES * b:LANES * (b + 1)]

    def swap_outer(last, carry):
        for a in halves:
            for b in halves:
                rows = pl.ds(LANES * a + last, SUBLANES, stride=SHELL)
                values = turned_ref[b, rows, :]
                rows = pl.ds(LANES * b + last, SUBLANES, stride=SHELL)
                last_ref[a, rows, :] = swap_groups(values)
        return carry

    lax.fori_loop(0, SHELL, swap_outer, 0, unroll=4)
    last = jnp.concatenate((last_ref[0], last_ref[1]), axis=1)
    keep(2, last)


def make_tables(class_tables):
    classes, width, _ = class_tables.shape
    return pl.pallas_call(
        table_kernel,
        grid=(classes,),
        out_shape=jax.ShapeDtypeStruct((classes, 3, 2, width, width), jnp.bfloat16),
        in_specs=[pl.BlockSpec((1, width, width), lambda c: (c, 0, 0))],
        out_specs=pl.BlockSpec((1, 3, 2, width, width), lambda c: (c, 0, 0, 0, 0)),
        scratch_shapes=[
            pltpu.VMEM((width, width), jnp.float32),
            pltpu.VMEM((2, width, LANES), jnp.float32),
            pltpu.VMEM((2, width, LANES), jnp.float32),
        ],
        compiler_params=pltpu.CompilerParams(vmem_limit_bytes=VMEM_BYTES),
        name="make_tables",
    )(class_tables)


def sort_kernel(count_ref, bra_ref, ket_ref, class_ref, factor_ref, columns_ref, rows_ref):
    slots = bra_ref.shape[1]
    bra, ket = bra_ref[...], ket_ref[...]
    shell_a, shell_b = bra // 32, bra % 32
    shell_c, shell_d = ket // 32, ket % 32
    slot = lax.broadcasted_iota(jnp.int32, (1, slots), 1)
    live = slot < count_ref[0]
    klass = jnp.where(live, class_ref[...], SUBLANES - 1)
    factor = jnp.where(live, factor_ref[...], 0.0)

    def line(first, second):
        return (((first // 2) * 16 + second // 2) * 4 + (first % 2) * 2 + second % 2).astype(jnp.float32)

    fields = jnp.concatenate(
        (
            line(shell_c, shell_d),
            line(shell_a, shell_b),
            line(shell_b, shell_d),
            line(shell_a, shell_c),
            line(shell_b, shell_c),
            line(shell_a, shell_d),
            klass.astype(jnp.float32),
            factor,
        ),
        axis=0,
    )
    number = lax.broadcasted_iota(jnp.int32, (SUBLANES, slots), 0)
    same = jnp.where(klass == number, 1.0, 0.0)
    start = jnp.sum(jnp.where(klass < number, 1.0, 0.0), axis=1, keepdims=True)
    low = lax.broadcasted_iota(jnp.int32, (slots, slots), 0)
    high = lax.broadcasted_iota(jnp.int32, (slots, slots), 1)
    before = jnp.where(low < high, 1.0, 0.0).astype(jnp.bfloat16)
    rank = dot(same.astype(jnp.bfloat16), before, NN) + start
    rank = jnp.sum(rank * same, axis=0, keepdims=True).astype(jnp.int32)
    order = jnp.where(low == rank, 1.0, 0.0)
    rows_ref[...] = lax.dot_general(
        fields, order, NT, precision=lax.Precision.HIGHEST, preferred_element_type=jnp.float32
    )
    columns_ref[...] = lax.dot_general(
        order, fields, NT, precision=lax.Precision.HIGHEST, preferred_element_type=jnp.float32
    )


def sort_quartets(count, bra, ket, klass, factor):
    slots = bra.shape[1]
    vmem = pl.BlockSpec(memory_space=pltpu.VMEM)
    return pl.pallas_call(
        sort_kernel,
        out_shape=(
            jax.ShapeDtypeStruct((slots, SUBLANES), jnp.float32),
            jax.ShapeDtypeStruct((SUBLANES, slots), jnp.float32),
        ),
        in_specs=[pl.BlockSpec(memory_space=pltpu.SMEM)] + [vmem] * 4,
        out_specs=(vmem, vmem),
        compiler_params=pltpu.CompilerParams(vmem_limit_bytes=VMEM_BYTES),
        name="sort_quartets",
    )(count, bra, ket, klass, factor)


STEP = 128


def quartet_kernel(
    ends_ref, blocks_ref, left_ref, right_ref, columns_ref, rows_ref, tables_ref,
    out_ref, scaled_ref, pieces_ref, totals_ref, found_ref, values_ref,
):
    classes = tables_ref.shape[0]
    pairs = pieces_ref.shape[0]
    width = totals_ref.shape[1]
    scaled_ref[...] = (blocks_ref[...].reshape(16, 16, SUBLANES, LANES) * left_ref[...][:, None]
                       * right_ref[...][None]).reshape(scaled_ref.shape)
    for half in range(2):
        high, low = split(scaled_ref[pl.ds(half, pairs, stride=2), :])
        pieces_ref[:, LANES * half:LANES * (half + 1)] = high
        pieces_ref[:, width + LANES * half:width + LANES * (half + 1)] = low
    totals_ref[...] = jnp.zeros_like(totals_ref)

    def step(index, carry):
        base = pl.multiple_of(index * STEP, STEP)
        here = pl.ds(base, STEP)
        columns = columns_ref[here, :]
        lane = lax.broadcasted_iota(jnp.int32, (STEP, pairs), 1)
        chosen = jnp.concatenate(
            [
                jnp.where(lane == columns[:, kind:kind + 1].astype(jnp.int32), 1.0, 0.0).astype(jnp.bfloat16)
                for kind in range(6)
            ],
            axis=0,
        )
        found = dot(chosen, pieces_ref[...], NN).astype(jnp.bfloat16)
        for kind in range(6):
            part = slice(STEP * kind, STEP * (kind + 1))
            found_ref[kind, :STEP] = found[part, :width]
            found_ref[kind, STEP:] = found[part, width:]
        values_ref[...] = jnp.zeros_like(values_ref)
        for klass in range(classes):
            begin = 0 if klass == 0 else ends_ref[klass - 1]

            @pl.when((begin < base + STEP) & (ends_ref[klass] > base) & (begin < ends_ref[klass]))
            def _():
                factor = jnp.where(columns[:, 6:7] == klass, columns[:, 7:8], 0.0)
                for kind in range(6):
                    part = slice(STEP * kind, STEP * (kind + 1))
                    dims = NT if kind % 2 == 0 else NN
                    product = dot(found_ref[kind], tables_ref[klass, kind // 2, 0], dims)
                    product = product[:STEP] + product[STEP:]
                    product += dot(found_ref[kind, :STEP], tables_ref[klass, kind // 2, 1], dims)
                    values_ref[part, :] += product * (factor if kind < 2 else -0.5 * factor)

        high, low = split(values_ref[...])
        sublane = lax.broadcasted_iota(jnp.int32, (pairs, STEP), 0)
        chosen = jnp.concatenate(
            [
                jnp.where(sublane == rows_ref[kind ^ 1:(kind ^ 1) + 1, here].astype(jnp.int32), 1.0, 0.0).astype(
                    jnp.bfloat16
                )
                for kind in range(6)
            ],
            axis=1,
        )
        totals_ref[...] += dot(chosen, high, NN) + dot(chosen, low, NN)
        return carry

    lax.fori_loop(0, (ends_ref[classes - 1] + STEP - 1) // STEP, step, 0)
    for half in range(2):
        scaled_ref[pl.ds(half, pairs, stride=2), :] = totals_ref[:, LANES * half:LANES * (half + 1)]
    out_ref[...] = (scaled_ref[...].reshape(16, 16, SUBLANES, LANES) * left_ref[...][:, None]
                    * right_ref[...][None]).reshape(out_ref.shape)


def add_quartets(ends, blocks, left, right, columns, rows, tables):
    lines = blocks.shape[0]
    width = tables.shape[-1]
    vmem = pl.BlockSpec(memory_space=pltpu.VMEM)
    return pl.pallas_call(
        quartet_kernel,
        out_shape=jax.ShapeDtypeStruct(blocks.shape, jnp.float32),
        in_specs=[pl.BlockSpec(memory_space=pltpu.SMEM)] + [vmem] * 6,
        out_specs=vmem,
        scratch_shapes=[
            pltpu.VMEM((lines, LANES), jnp.float32),
            pltpu.VMEM((lines // 2, 2 * width), jnp.bfloat16),
            pltpu.VMEM((lines // 2, width), jnp.float32),
            pltpu.VMEM((6, 2 * STEP, width), jnp.bfloat16),
            pltpu.VMEM((6 * STEP, width), jnp.float32),
        ],
        compiler_params=pltpu.CompilerParams(vmem_limit_bytes=VMEM_BYTES),
        name="add_quartets",
    )(ends, blocks, left, right, columns, rows, tables)


def exchange(values):
    return lax.all_to_all(values, AXES, split_axis=0, concat_axis=0, tiled=True)


def on_device(
    density,
    core_hamiltonian,
    class_tables,
    shell_scale,
    block_place,
    work_blocks,
    quartet_bra,
    quartet_ket,
    quartet_class,
    quartet_factor,
    quartet_count,
):
    row_count = lax.axis_size("row")
    col_count = lax.axis_size("col")
    devices = row_count * col_count
    row_blocks = density.shape[0] // SHELL
    col_blocks = density.shape[1] // SHELL
    classes = class_tables.shape[0]
    own_tasks = work_blocks[0]
    places = block_place[own_tasks]
    row_part = (places % row_blocks * (2 * col_blocks)).reshape(row_count, 2)
    col_part = (places % col_blocks * 2).reshape(col_count, 2)
    outgoing = jnp.concatenate(
        (
            jnp.broadcast_to(row_part[:, None, :], (row_count, col_count, 2)),
            jnp.broadcast_to(col_part[None, :, :], (row_count, col_count, 2)),
        ),
        axis=2,
    )
    wanted = exchange(outgoing.reshape(devices, 1, 4))
    picked = pick_blocks(wanted, flatten_blocks(density), devices)
    blocks = exchange(picked.reshape(devices, SUBLANES, LANES))
    blocks = blocks.reshape(devices * SUBLANES, LANES)

    tables = make_tables(class_tables)
    scales = shell_scale.reshape(-1, SHELL)[own_tasks]
    left = jnp.broadcast_to(
        scales.reshape(row_count, 2, 1, 2, SUBLANES, 1), (row_count, 2, 2, 2, SUBLANES, SHELL)
    ).reshape(row_count, SUBLANES, LANES)
    right = jnp.broadcast_to(
        scales.reshape(col_count, 1, 2, 1, 1, SHELL), (col_count, 2, 2, 2, SUBLANES, SHELL)
    ).reshape(col_count, SUBLANES, LANES)
    columns, rows = sort_quartets(quartet_count, quartet_bra, quartet_ket, quartet_class, quartet_factor)
    slots = quartet_class.shape[1]
    within = jnp.where(jnp.arange(slots) < quartet_count[0], quartet_class[0], classes)
    ends = jnp.sum((within[None, :] <= jnp.arange(classes)[:, None]).astype(jnp.int32), axis=1)
    summed = add_quartets(ends, blocks, left, right, columns, rows, tables)
    returned = exchange(summed.reshape(devices, SUBLANES, LANES))
    return merge_blocks(wanted, returned.reshape(devices * SUBLANES, LANES), core_hamiltonian)


def solution(mesh):
    placed = (
        P("row", "col"),
        P("row", "col"),
        P(),
        P(),
        P(),
        P(("row", "col"), None),
        P(("row", "col"), None),
        P(("row", "col"), None),
        P(("row", "col"), None),
        P(("row", "col"), None),
        P(("row", "col")),
    )
    return jax.shard_map(
        on_device, mesh=mesh, in_specs=placed, out_specs=P("row", "col"), check_vma=False
    )
```

```python
import functools

import jax
import jax.numpy as jnp
from jax import lax
from jax.experimental import pallas as pl
from jax.experimental.pallas import tpu as pltpu
from jax.sharding import PartitionSpec as P

SHELL = 16
LANES = 128
SUBLANES = 8
STRIPE = 40
VMEM_BYTES = 16 << 20
GROUPS = LANES // SHELL
AXES = ("row", "col")
NT = (((1,), (1,)), ((), ()))
NN = (((1,), (0,)), ((), ()))


def swap_groups(tile):
    sublane = lax.broadcasted_iota(jnp.int32, tile.shape, 0)
    lane = lax.broadcasted_iota(jnp.int32, tile.shape, 1)
    group, inner = lane // SHELL, lane % SHELL
    tile = jnp.take_along_axis(tile, ((sublane + group) % GROUPS) * SHELL + inner, axis=1)
    tile = jnp.take_along_axis(tile, (sublane - group) % SUBLANES, axis=0)
    return jnp.take_along_axis(tile, ((sublane - group) % GROUPS) * SHELL + inner, axis=1)


def split(values):
    high = values.astype(jnp.bfloat16)
    low = (values - high.astype(jnp.float32)).astype(jnp.bfloat16)
    return high, low


def dot(left, right, dims):
    return lax.dot_general(left, right, dims, preferred_element_type=jnp.float32)


def ask_kernel(work_ref, place_ref, out_ref):
    tasks = work_ref.shape[1]
    devices = out_ref.shape[0]
    row = lax.broadcasted_iota(jnp.int32, (tasks, tasks), 0)
    lane = lax.broadcasted_iota(jnp.int32, (tasks, tasks), 1)
    work = jnp.sum(jnp.where(row == lane, work_ref[...], 0).astype(jnp.float32), axis=1, keepdims=True)
    work = work.astype(jnp.int32)
    lane = lax.broadcasted_iota(jnp.int32, (tasks, LANES), 1)
    table = jnp.zeros((tasks, LANES), jnp.float32)
    for part in range(place_ref.shape[0]):
        hit = work == lane + part * LANES
        table += jnp.where(hit, place_ref[part:part + 1, :], 0).astype(jnp.float32)
    place = jnp.sum(table, axis=1, keepdims=True).astype(jnp.int32) % STRIPE
    first = (place * (2 * STRIPE)).astype(jnp.float32)
    second = (place * 2).astype(jnp.float32)
    values = jnp.concatenate((first, first, second, second), axis=0)
    row = lax.broadcasted_iota(jnp.int32, (4 * tasks, LANES), 0)
    lane = lax.broadcasted_iota(jnp.int32, (4 * tasks, LANES), 1)
    values = jnp.where(lane == row // tasks, values, 0.0)
    owner = lax.broadcasted_iota(jnp.int32, (devices, 4 * tasks), 0)
    place = lax.broadcasted_iota(jnp.int32, (devices, 4 * tasks), 1)
    part, task = place // tasks, place % tasks
    index = jnp.where(part < 2, owner // (tasks // 2), owner % (tasks // 2))
    chosen = jnp.where(task == 2 * index + part % 2, 1.0, 0.0)
    asked = lax.dot_general(
        chosen, values, NN, precision=lax.Precision.HIGHEST, preferred_element_type=jnp.float32
    )
    out_ref[...] = asked.astype(jnp.int32)


def ask_blocks(work_blocks, block_place, devices):
    return pl.pallas_call(
        ask_kernel,
        out_shape=jax.ShapeDtypeStruct((devices, LANES), jnp.int32),
        compiler_params=pltpu.CompilerParams(vmem_limit_bytes=VMEM_BYTES),
        name="ask_blocks",
    )(work_blocks, block_place.reshape(-1, LANES))


def flatten_kernel(density_ref, flat_ref):
    row_blocks = density_ref.shape[0] // SHELL
    col_blocks = density_ref.shape[1] // SHELL

    def flatten(block, carry):
        for half in range(2):
            start = pl.multiple_of(block * SHELL + half * SUBLANES, SUBLANES)
            for tile in range(col_blocks // GROUPS):
                lanes = slice(tile * LANES, (tile + 1) * LANES)
                values = density_ref[pl.ds(start, SUBLANES), lanes]
                place = (block * col_blocks + tile * GROUPS) * 2 + half
                flat_ref[pl.ds(place, SUBLANES, stride=2), :] = swap_groups(values)
        return carry

    lax.fori_loop(0, row_blocks, flatten, 0, unroll=8)


def flatten_blocks(density):
    blocks = (density.shape[0] // SHELL) * (density.shape[1] // SHELL)
    return pl.pallas_call(
        flatten_kernel,
        out_shape=jax.ShapeDtypeStruct((2 * blocks, LANES), jnp.float32),
        compiler_params=pltpu.CompilerParams(vmem_limit_bytes=VMEM_BYTES),
        name="flatten_blocks",
    )(density)


def pick_kernel(wanted_ref, flat_ref, out_ref, lines_ref, turned_ref, scalars_ref, arrived):
    devices = lines_ref.shape[1]
    turned = wanted_ref[...].T
    turned_ref[...] = jnp.concatenate(
        [turned[part // 2:part // 2 + 1] + turned[2 + part % 2:3 + part % 2] for part in range(4)] * 2, axis=0
    )
    copy = pltpu.make_async_copy(turned_ref, scalars_ref, arrived)
    copy.start()
    lines_ref[...] = turned_ref[...]
    copy.wait()

    def pick(device, carry):
        for part in range(4):
            source = pl.multiple_of(scalars_ref[part, device], 2)
            target = pl.multiple_of(SUBLANES * device + 2 * part, 2)
            out_ref[pl.ds(target, 2), :] = flat_ref[pl.ds(source, 2), :]
        return carry

    lax.fori_loop(0, devices, pick, 0, unroll=8)


def pick_blocks(wanted, flat):
    devices = wanted.shape[0]
    return pl.pallas_call(
        pick_kernel,
        out_shape=(
            jax.ShapeDtypeStruct((devices * SUBLANES, LANES), jnp.float32),
            jax.ShapeDtypeStruct((SUBLANES, devices), jnp.int32),
        ),
        scratch_shapes=[
            pltpu.VMEM((SUBLANES, devices), jnp.int32),
            pltpu.SMEM((SUBLANES, devices), jnp.int32),
            pltpu.SemaphoreType.DMA,
        ],
        compiler_params=pltpu.CompilerParams(vmem_limit_bytes=VMEM_BYTES),
        name="pick_blocks",
    )(wanted, flat)


def merge_kernel(wanted_ref, parts_ref, core_ref, out_ref, flat_ref):
    row_blocks = core_ref.shape[0] // SHELL
    col_blocks = core_ref.shape[1] // SHELL
    devices = parts_ref.shape[0] // SUBLANES
    flat_ref[...] = jnp.zeros_like(flat_ref)

    def add(device, carry):
        places = []
        sums = []
        for part in range(4):
            place = pl.ds(pl.multiple_of(wanted_ref[part, device], 2), 2)
            source = pl.multiple_of(SUBLANES * device + 2 * part, 2)
            places.append(place)
            sums.append(flat_ref[place, :] + parts_ref[pl.ds(source, 2), :])
        for place, value in zip(places, sums):
            flat_ref[place, :] = value
        return carry

    lax.fori_loop(0, devices, add, 0, unroll=8)

    def unflatten(block, carry):
        for half in range(2):
            start = pl.multiple_of(block * SHELL + half * SUBLANES, SUBLANES)
            for tile in range(col_blocks // GROUPS):
                lanes = slice(tile * LANES, (tile + 1) * LANES)
                place = (block * col_blocks + tile * GROUPS) * 2 + half
                values = swap_groups(flat_ref[pl.ds(place, SUBLANES, stride=2), :])
                out_ref[pl.ds(start, SUBLANES), lanes] = core_ref[pl.ds(start, SUBLANES), lanes] + values
        return carry

    lax.fori_loop(0, row_blocks, unflatten, 0, unroll=8)


def merge_blocks(wanted, parts, core):
    blocks = (core.shape[0] // SHELL) * (core.shape[1] // SHELL)
    return pl.pallas_call(
        merge_kernel,
        out_shape=jax.ShapeDtypeStruct(core.shape, jnp.float32),
        in_specs=[
            pl.BlockSpec(memory_space=pltpu.SMEM),
            pl.BlockSpec(memory_space=pltpu.VMEM),
            pl.BlockSpec(memory_space=pltpu.VMEM),
        ],
        out_specs=pl.BlockSpec(memory_space=pltpu.VMEM),
        scratch_shapes=[pltpu.VMEM((2 * blocks, LANES), jnp.float32)],
        compiler_params=pltpu.CompilerParams(vmem_limit_bytes=VMEM_BYTES),
        name="merge_blocks",
    )(wanted, parts, core)


def table_kernel(tables_ref, out_ref, mid_ref, turned_ref, last_ref):
    width = tables_ref.shape[1]
    halves = range(2)

    def keep(form, values):
        out_ref[0, form, 0], out_ref[0, form, 1] = split(values)

    keep(0, tables_ref[0])

    def swap_inner(first, carry):
        for a in halves:
            for b in halves:
                rows = pl.ds(pl.multiple_of(first * SHELL + SUBLANES * a, SUBLANES), SUBLANES)
                values = tables_ref[0, rows, LANES * b:LANES * (b + 1)]
                rows = pl.ds(pl.multiple_of(first * SHELL + SUBLANES * b, SUBLANES), SUBLANES)
                mid_ref[rows, LANES * a:LANES * (a + 1)] = swap_groups(values)
        return carry

    lax.fori_loop(0, width // SHELL, swap_inner, 0, unroll=4)
    turned = mid_ref[...].T
    keep(1, mid_ref[...])
    for b in halves:
        turned_ref[b] = turned[:, LANES * b:LANES * (b + 1)]

    def swap_outer(last, carry):
        for a in halves:
            for b in halves:
                rows = pl.ds(LANES * a + last, SUBLANES, stride=SHELL)
                values = turned_ref[b, rows, :]
                rows = pl.ds(LANES * b + last, SUBLANES, stride=SHELL)
                last_ref[a, rows, :] = swap_groups(values)
        return carry

    lax.fori_loop(0, SHELL, swap_outer, 0, unroll=4)
    last = jnp.concatenate((last_ref[0], last_ref[1]), axis=1)
    keep(2, last)


def make_tables(class_tables):
    classes, width, _ = class_tables.shape
    return pl.pallas_call(
        table_kernel,
        grid=(classes,),
        out_shape=jax.ShapeDtypeStruct((classes, 3, 2, width, width), jnp.bfloat16),
        in_specs=[pl.BlockSpec((1, width, width), lambda c: (c, 0, 0))],
        out_specs=pl.BlockSpec((1, 3, 2, width, width), lambda c: (c, 0, 0, 0, 0)),
        scratch_shapes=[
            pltpu.VMEM((width, width), jnp.float32),
            pltpu.VMEM((2, width, LANES), jnp.float32),
            pltpu.VMEM((2, width, LANES), jnp.float32),
        ],
        compiler_params=pltpu.CompilerParams(vmem_limit_bytes=VMEM_BYTES),
        name="make_tables",
    )(class_tables)


def sort_kernel(count_ref, bra_ref, ket_ref, class_ref, factor_ref, rows_ref):
    slots = bra_ref.shape[1]
    bra, ket = bra_ref[...], ket_ref[...]
    shell_a, shell_b = bra // 32, bra % 32
    shell_c, shell_d = ket // 32, ket % 32
    slot = lax.broadcasted_iota(jnp.int32, (1, slots), 1)
    live = slot < count_ref[0]
    klass = jnp.where(live, class_ref[...], SUBLANES - 1)
    factor = jnp.where(live, factor_ref[...], 0.0)

    def line(first, second):
        return (((first // 2) * 16 + second // 2) * 4 + (first % 2) * 2 + second % 2).astype(jnp.float32)

    fields = jnp.concatenate(
        (
            line(shell_c, shell_d),
            line(shell_a, shell_b),
            line(shell_b, shell_d),
            line(shell_a, shell_c),
            line(shell_b, shell_c),
            line(shell_a, shell_d),
            klass.astype(jnp.float32),
            factor,
        ),
        axis=0,
    )
    number = lax.broadcasted_iota(jnp.int32, (SUBLANES, slots), 0)
    same = jnp.where(klass == number, 1.0, 0.0)
    start = jnp.sum(jnp.where(klass < number, 1.0, 0.0), axis=1, keepdims=True)
    low = lax.broadcasted_iota(jnp.int32, (slots, slots), 0)
    high = lax.broadcasted_iota(jnp.int32, (slots, slots), 1)
    before = jnp.where(low < high, 1.0, 0.0).astype(jnp.bfloat16)
    rank = dot(same.astype(jnp.bfloat16), before, NN) + start
    rank = jnp.sum(rank * same, axis=0, keepdims=True).astype(jnp.int32)
    order = jnp.where(low == rank, 1.0, 0.0)
    rows_ref[...] = lax.dot_general(
        fields, order, NT, precision=lax.Precision.HIGHEST, preferred_element_type=jnp.float32
    )


def sort_quartets(count, bra, ket, klass, factor):
    slots = bra.shape[1]
    vmem = pl.BlockSpec(memory_space=pltpu.VMEM)
    return pl.pallas_call(
        sort_kernel,
        out_shape=jax.ShapeDtypeStruct((SUBLANES, slots), jnp.float32),
        in_specs=[pl.BlockSpec(memory_space=pltpu.SMEM)] + [vmem] * 4,
        out_specs=vmem,
        compiler_params=pltpu.CompilerParams(vmem_limit_bytes=VMEM_BYTES),
        name="sort_quartets",
    )(count, bra, ket, klass, factor)


STEP = 128


def quartet_kernel(
    ends_ref, blocks_ref, left_ref, right_ref, rows_ref, tables_ref,
    out_ref, scaled_ref, pieces_ref, totals_ref, found_ref, values_ref,
):
    classes = tables_ref.shape[0]
    pairs = pieces_ref.shape[0]
    width = totals_ref.shape[1]
    scaled_ref[...] = (blocks_ref[...].reshape(16, 16, SUBLANES, LANES) * left_ref[...][:, None]
                       * right_ref[...][None]).reshape(scaled_ref.shape)
    for half in range(2):
        high, low = split(scaled_ref[pl.ds(half, pairs, stride=2), :])
        pieces_ref[:, LANES * half:LANES * (half + 1)] = high
        pieces_ref[:, width + LANES * half:width + LANES * (half + 1)] = low
    totals_ref[...] = jnp.zeros_like(totals_ref)

    def step(index, carry):
        base = pl.multiple_of(index * STEP, STEP)
        here = pl.ds(base, STEP)
        columns = rows_ref[:, here].T
        lane = lax.broadcasted_iota(jnp.int32, (STEP, pairs), 1)
        chosen = jnp.concatenate(
            [
                jnp.where(lane == columns[:, kind:kind + 1].astype(jnp.int32), 1.0, 0.0).astype(jnp.bfloat16)
                for kind in range(6)
            ],
            axis=0,
        )
        found = dot(chosen, pieces_ref[...], NN).astype(jnp.bfloat16)
        for kind in range(6):
            part = slice(STEP * kind, STEP * (kind + 1))
            found_ref[kind, :STEP] = found[part, :width]
            found_ref[kind, STEP:] = found[part, width:]
        values_ref[...] = jnp.zeros_like(values_ref)
        for klass in range(classes):
            begin = 0 if klass == 0 else ends_ref[klass - 1]

            @pl.when((begin < base + STEP) & (ends_ref[klass] > base) & (begin < ends_ref[klass]))
            def _():
                factor = jnp.where(columns[:, 6:7] == klass, columns[:, 7:8], 0.0)
                for kind in range(6):
                    part = slice(STEP * kind, STEP * (kind + 1))
                    dims = NT if kind % 2 == 0 else NN
                    product = dot(found_ref[kind], tables_ref[klass, kind // 2, 0], dims)
                    product = product[:STEP] + product[STEP:]
                    product += dot(found_ref[kind, :STEP], tables_ref[klass, kind // 2, 1], dims)
                    values_ref[part, :] += product * (factor if kind < 2 else -0.5 * factor)

        high, low = split(values_ref[...])
        sublane = lax.broadcasted_iota(jnp.int32, (pairs, STEP), 0)
        chosen = jnp.concatenate(
            [
                jnp.where(sublane == rows_ref[kind ^ 1:(kind ^ 1) + 1, here].astype(jnp.int32), 1.0, 0.0).astype(
                    jnp.bfloat16
                )
                for kind in range(6)
            ],
            axis=1,
        )
        totals_ref[...] += dot(chosen, high, NN) + dot(chosen, low, NN)
        return carry

    lax.fori_loop(0, (ends_ref[classes - 1] + STEP - 1) // STEP, step, 0)
    for half in range(2):
        scaled_ref[pl.ds(half, pairs, stride=2), :] = totals_ref[:, LANES * half:LANES * (half + 1)]
    out_ref[...] = (scaled_ref[...].reshape(16, 16, SUBLANES, LANES) * left_ref[...][:, None]
                    * right_ref[...][None]).reshape(out_ref.shape)


def add_quartets(ends, blocks, left, right, rows, tables):
    lines = blocks.shape[0]
    width = tables.shape[-1]
    vmem = pl.BlockSpec(memory_space=pltpu.VMEM)
    return pl.pallas_call(
        quartet_kernel,
        out_shape=jax.ShapeDtypeStruct(blocks.shape, jnp.float32),
        in_specs=[pl.BlockSpec(memory_space=pltpu.SMEM)] + [vmem] * 5,
        out_specs=vmem,
        scratch_shapes=[
            pltpu.VMEM((lines, LANES), jnp.float32),
            pltpu.VMEM((lines // 2, 2 * width), jnp.bfloat16),
            pltpu.VMEM((lines // 2, width), jnp.float32),
            pltpu.VMEM((6, 2 * STEP, width), jnp.bfloat16),
            pltpu.VMEM((6 * STEP, width), jnp.float32),
        ],
        compiler_params=pltpu.CompilerParams(vmem_limit_bytes=VMEM_BYTES),
        name="add_quartets",
    )(ends, blocks, left, right, rows, tables)


def exchange(values):
    return lax.all_to_all(values, AXES, split_axis=0, concat_axis=0, tiled=True)


def on_device(
    density,
    core_hamiltonian,
    class_tables,
    shell_scale,
    block_place,
    work_blocks,
    quartet_bra,
    quartet_ket,
    quartet_class,
    quartet_factor,
    quartet_count,
):
    row_count = lax.axis_size("row")
    col_count = lax.axis_size("col")
    devices = row_count * col_count
    classes = class_tables.shape[0]
    own_tasks = work_blocks[0]
    asked = ask_blocks(work_blocks, block_place, devices)
    wanted = exchange(asked.reshape(devices, 1, LANES)).reshape(devices, LANES)
    picked, lines = pick_blocks(wanted, flatten_blocks(density))
    blocks = exchange(picked.reshape(devices, SUBLANES, LANES))
    blocks = blocks.reshape(devices * SUBLANES, LANES)

    tables = make_tables(class_tables)
    scales = shell_scale.reshape(-1, SHELL)[own_tasks]
    left = jnp.broadcast_to(
        scales.reshape(row_count, 2, 1, 2, SUBLANES, 1), (row_count, 2, 2, 2, SUBLANES, SHELL)
    ).reshape(row_count, SUBLANES, LANES)
    right = jnp.broadcast_to(
        scales.reshape(col_count, 1, 2, 1, 1, SHELL), (col_count, 2, 2, 2, SUBLANES, SHELL)
    ).reshape(col_count, SUBLANES, LANES)
    rows = sort_quartets(quartet_count, quartet_bra, quartet_ket, quartet_class, quartet_factor)
    slots = quartet_class.shape[1]
    within = jnp.where(jnp.arange(slots) < quartet_count[0], quartet_class[0], classes)
    ends = jnp.sum((within[None, :] <= jnp.arange(classes)[:, None]).astype(jnp.int32), axis=1)
    summed = add_quartets(ends, blocks, left, right, rows, tables)
    returned = exchange(summed.reshape(devices, SUBLANES, LANES))
    return merge_blocks(lines, returned.reshape(devices * SUBLANES, LANES), core_hamiltonian)


def solution(mesh):
    placed = (
        P("row", "col"),
        P("row", "col"),
        P(),
        P(),
        P(),
        P(("row", "col"), None),
        P(("row", "col"), None),
        P(("row", "col"), None),
        P(("row", "col"), None),
        P(("row", "col"), None),
        P(("row", "col")),
    )
    return jax.shard_map(
        on_device, mesh=mesh, in_specs=placed, out_specs=P("row", "col"), check_vma=False
    )
```

```python
import functools

import jax
import jax.numpy as jnp
from jax import lax
from jax.experimental import pallas as pl
from jax.experimental.pallas import tpu as pltpu
from jax.sharding import PartitionSpec as P

SHELL = 16
LANES = 128
SUBLANES = 8
STRIPE = 40
VMEM_BYTES = 24 << 20
GROUPS = LANES // SHELL
AXES = ("row", "col")
NT = (((1,), (1,)), ((), ()))
NN = (((1,), (0,)), ((), ()))


def swap_groups(tile):
    sublane = lax.broadcasted_iota(jnp.int32, tile.shape, 0)
    lane = lax.broadcasted_iota(jnp.int32, tile.shape, 1)
    group, inner = lane // SHELL, lane % SHELL
    tile = jnp.take_along_axis(tile, ((sublane + group) % GROUPS) * SHELL + inner, axis=1)
    tile = jnp.take_along_axis(tile, (sublane - group) % SUBLANES, axis=0)
    return jnp.take_along_axis(tile, ((sublane - group) % GROUPS) * SHELL + inner, axis=1)


def split(values):
    high = values.astype(jnp.bfloat16)
    low = (values - high.astype(jnp.float32)).astype(jnp.bfloat16)
    return high, low


def dot(left, right, dims):
    return lax.dot_general(left, right, dims, preferred_element_type=jnp.float32)


def ask_kernel(work_ref, place_ref, out_ref):
    tasks = work_ref.shape[1]
    devices = out_ref.shape[0]
    row = lax.broadcasted_iota(jnp.int32, (tasks, tasks), 0)
    lane = lax.broadcasted_iota(jnp.int32, (tasks, tasks), 1)
    work = jnp.sum(jnp.where(row == lane, work_ref[...], 0).astype(jnp.float32), axis=1, keepdims=True)
    work = work.astype(jnp.int32)
    lane = lax.broadcasted_iota(jnp.int32, (tasks, LANES), 1)
    table = jnp.zeros((tasks, LANES), jnp.float32)
    for part in range(place_ref.shape[0]):
        hit = work == lane + part * LANES
        table += jnp.where(hit, place_ref[part:part + 1, :], 0).astype(jnp.float32)
    place = jnp.sum(table, axis=1, keepdims=True).astype(jnp.int32) % STRIPE
    first = (place * (2 * STRIPE)).astype(jnp.float32)
    second = (place * 2).astype(jnp.float32)
    values = jnp.concatenate((first, first, second, second), axis=0)
    row = lax.broadcasted_iota(jnp.int32, (4 * tasks, LANES), 0)
    lane = lax.broadcasted_iota(jnp.int32, (4 * tasks, LANES), 1)
    values = jnp.where(lane == row // tasks, values, 0.0)
    owner = lax.broadcasted_iota(jnp.int32, (devices, 4 * tasks), 0)
    place = lax.broadcasted_iota(jnp.int32, (devices, 4 * tasks), 1)
    part, task = place // tasks, place % tasks
    index = jnp.where(part < 2, owner // (tasks // 2), owner % (tasks // 2))
    chosen = jnp.where(task == 2 * index + part % 2, 1.0, 0.0)
    asked = lax.dot_general(
        chosen, values, NN, precision=lax.Precision.HIGHEST, preferred_element_type=jnp.float32
    )
    out_ref[...] = asked.astype(jnp.int32)


def ask_blocks(work_blocks, block_place, devices):
    return pl.pallas_call(
        ask_kernel,
        out_shape=jax.ShapeDtypeStruct((devices, LANES), jnp.int32),
        compiler_params=pltpu.CompilerParams(vmem_limit_bytes=60 << 20),
        name="ask_blocks",
    )(work_blocks, block_place.reshape(-1, LANES))


def flatten_kernel(density_ref, flat_ref):
    row_blocks = density_ref.shape[0] // SHELL
    col_blocks = density_ref.shape[1] // SHELL

    def flatten(block, carry):
        for half in range(2):
            start = pl.multiple_of(block * SHELL + half * SUBLANES, SUBLANES)
            for tile in range(col_blocks // GROUPS):
                lanes = slice(tile * LANES, (tile + 1) * LANES)
                values = density_ref[pl.ds(start, SUBLANES), lanes]
                place = (block * col_blocks + tile * GROUPS) * 2 + half
                flat_ref[pl.ds(place, SUBLANES, stride=2), :] = swap_groups(values)
        return carry

    lax.fori_loop(0, row_blocks, flatten, 0, unroll=8)


def flatten_blocks(density):
    blocks = (density.shape[0] // SHELL) * (density.shape[1] // SHELL)
    return pl.pallas_call(
        flatten_kernel,
        out_shape=jax.ShapeDtypeStruct((2 * blocks, LANES), jnp.float32),
        compiler_params=pltpu.CompilerParams(vmem_limit_bytes=VMEM_BYTES),
        name="flatten_blocks",
    )(density)


def pick_kernel(wanted_ref, flat_ref, out_ref, lines_ref, turned_ref, scalars_ref, arrived):
    devices = lines_ref.shape[1]
    turned = wanted_ref[...].T
    turned_ref[...] = jnp.concatenate(
        [turned[part // 2:part // 2 + 1] + turned[2 + part % 2:3 + part % 2] for part in range(4)] * 2, axis=0
    )
    copy = pltpu.make_async_copy(turned_ref, scalars_ref, arrived)
    copy.start()
    lines_ref[...] = turned_ref[...]
    copy.wait()

    def pick(device, carry):
        for part in range(4):
            source = pl.multiple_of(scalars_ref[part, device], 2)
            target = pl.multiple_of(SUBLANES * device + 2 * part, 2)
            out_ref[pl.ds(target, 2), :] = flat_ref[pl.ds(source, 2), :]
        return carry

    lax.fori_loop(0, devices, pick, 0, unroll=8)


def pick_blocks(wanted, flat):
    devices = wanted.shape[0]
    return pl.pallas_call(
        pick_kernel,
        out_shape=(
            jax.ShapeDtypeStruct((devices * SUBLANES, LANES), jnp.float32),
            jax.ShapeDtypeStruct((SUBLANES, devices), jnp.int32),
        ),
        scratch_shapes=[
            pltpu.VMEM((SUBLANES, devices), jnp.int32),
            pltpu.SMEM((SUBLANES, devices), jnp.int32),
            pltpu.SemaphoreType.DMA,
        ],
        compiler_params=pltpu.CompilerParams(vmem_limit_bytes=VMEM_BYTES),
        name="pick_blocks",
    )(wanted, flat)


def merge_kernel(wanted_ref, parts_ref, core_ref, out_ref, flat_ref):
    row_blocks = core_ref.shape[0] // SHELL
    col_blocks = core_ref.shape[1] // SHELL
    devices = parts_ref.shape[0] // SUBLANES
    flat_ref[...] = jnp.zeros_like(flat_ref)

    def add(device, carry):
        places = []
        sums = []
        for part in range(4):
            place = pl.ds(pl.multiple_of(wanted_ref[part, device], 2), 2)
            source = pl.multiple_of(SUBLANES * device + 2 * part, 2)
            places.append(place)
            sums.append(flat_ref[place, :] + parts_ref[pl.ds(source, 2), :])
        for place, value in zip(places, sums):
            flat_ref[place, :] = value
        return carry

    lax.fori_loop(0, devices, add, 0, unroll=8)

    def unflatten(block, carry):
        for half in range(2):
            start = pl.multiple_of(block * SHELL + half * SUBLANES, SUBLANES)
            for tile in range(col_blocks // GROUPS):
                lanes = slice(tile * LANES, (tile + 1) * LANES)
                place = (block * col_blocks + tile * GROUPS) * 2 + half
                values = swap_groups(flat_ref[pl.ds(place, SUBLANES, stride=2), :])
                out_ref[pl.ds(start, SUBLANES), lanes] = core_ref[pl.ds(start, SUBLANES), lanes] + values
        return carry

    lax.fori_loop(0, row_blocks, unflatten, 0, unroll=8)


def merge_blocks(wanted, parts, core):
    blocks = (core.shape[0] // SHELL) * (core.shape[1] // SHELL)
    return pl.pallas_call(
        merge_kernel,
        out_shape=jax.ShapeDtypeStruct(core.shape, jnp.float32),
        in_specs=[
            pl.BlockSpec(memory_space=pltpu.SMEM),
            pl.BlockSpec(memory_space=pltpu.VMEM),
            pl.BlockSpec(memory_space=pltpu.VMEM),
        ],
        out_specs=pl.BlockSpec(memory_space=pltpu.VMEM),
        scratch_shapes=[pltpu.VMEM((2 * blocks, LANES), jnp.float32)],
        compiler_params=pltpu.CompilerParams(vmem_limit_bytes=VMEM_BYTES),
        name="merge_blocks",
    )(wanted, parts, core)


def table_kernel(tables_ref, out_ref, mid_ref, turned_ref, last_ref):
    width = tables_ref.shape[1]
    halves = range(2)

    def keep(form, values):
        out_ref[0, form, 0], out_ref[0, form, 1] = split(values)

    keep(0, tables_ref[0])

    def swap_inner(first, carry):
        for a in halves:
            for b in halves:
                rows = pl.ds(pl.multiple_of(first * SHELL + SUBLANES * a, SUBLANES), SUBLANES)
                values = tables_ref[0, rows, LANES * b:LANES * (b + 1)]
                rows = pl.ds(pl.multiple_of(first * SHELL + SUBLANES * b, SUBLANES), SUBLANES)
                mid_ref[rows, LANES * a:LANES * (a + 1)] = swap_groups(values)
        return carry

    lax.fori_loop(0, width // SHELL, swap_inner, 0, unroll=4)
    turned = mid_ref[...].T
    keep(1, mid_ref[...])
    for b in halves:
        turned_ref[b] = turned[:, LANES * b:LANES * (b + 1)]

    def swap_outer(last, carry):
        for a in halves:
            for b in halves:
                rows = pl.ds(LANES * a + last, SUBLANES, stride=SHELL)
                values = turned_ref[b, rows, :]
                rows = pl.ds(LANES * b + last, SUBLANES, stride=SHELL)
                last_ref[a, rows, :] = swap_groups(values)
        return carry

    lax.fori_loop(0, SHELL, swap_outer, 0, unroll=4)
    last = jnp.concatenate((last_ref[0], last_ref[1]), axis=1)
    keep(2, last)


def make_tables(class_tables):
    classes, width, _ = class_tables.shape
    return pl.pallas_call(
        table_kernel,
        grid=(classes,),
        out_shape=jax.ShapeDtypeStruct((classes, 3, 2, width, width), jnp.bfloat16),
        in_specs=[pl.BlockSpec((1, width, width), lambda c: (c, 0, 0))],
        out_specs=pl.BlockSpec((1, 3, 2, width, width), lambda c: (c, 0, 0, 0, 0)),
        scratch_shapes=[
            pltpu.VMEM((width, width), jnp.float32),
            pltpu.VMEM((2, width, LANES), jnp.float32),
            pltpu.VMEM((2, width, LANES), jnp.float32),
        ],
        compiler_params=pltpu.CompilerParams(vmem_limit_bytes=VMEM_BYTES),
        name="make_tables",
    )(class_tables)


def sort_kernel(count_ref, bra_ref, ket_ref, class_ref, factor_ref, rows_ref):
    slots = bra_ref.shape[1]
    bra, ket = bra_ref[...], ket_ref[...]
    shell_a, shell_b = bra // 32, bra % 32
    shell_c, shell_d = ket // 32, ket % 32
    slot = lax.broadcasted_iota(jnp.int32, (1, slots), 1)
    live = slot < count_ref[0]
    klass = jnp.where(live, class_ref[...], SUBLANES - 1)
    factor = jnp.where(live, factor_ref[...], 0.0)

    def line(first, second):
        return (((first // 2) * 16 + second // 2) * 4 + (first % 2) * 2 + second % 2).astype(jnp.float32)

    fields = jnp.concatenate(
        (
            line(shell_c, shell_d),
            line(shell_a, shell_b),
            line(shell_b, shell_d),
            line(shell_a, shell_c),
            line(shell_b, shell_c),
            line(shell_a, shell_d),
            klass.astype(jnp.float32),
            factor,
        ),
        axis=0,
    )
    number = lax.broadcasted_iota(jnp.int32, (SUBLANES, slots), 0)
    same = jnp.where(klass == number, 1.0, 0.0)
    start = jnp.sum(jnp.where(klass < number, 1.0, 0.0), axis=1, keepdims=True)
    low = lax.broadcasted_iota(jnp.int32, (slots, slots), 0)
    high = lax.broadcasted_iota(jnp.int32, (slots, slots), 1)
    before = jnp.where(low < high, 1.0, 0.0).astype(jnp.bfloat16)
    rank = dot(same.astype(jnp.bfloat16), before, NN) + start
    rank = jnp.sum(rank * same, axis=0, keepdims=True).astype(jnp.int32)
    order = jnp.where(low == rank, 1.0, 0.0)
    rows_ref[...] = lax.dot_general(
        fields, order, NT, precision=lax.Precision.HIGHEST, preferred_element_type=jnp.float32
    )


def sort_quartets(count, bra, ket, klass, factor):
    slots = bra.shape[1]
    vmem = pl.BlockSpec(memory_space=pltpu.VMEM)
    return pl.pallas_call(
        sort_kernel,
        out_shape=jax.ShapeDtypeStruct((SUBLANES, slots), jnp.float32),
        in_specs=[pl.BlockSpec(memory_space=pltpu.SMEM)] + [vmem] * 4,
        out_specs=vmem,
        compiler_params=pltpu.CompilerParams(vmem_limit_bytes=VMEM_BYTES),
        name="sort_quartets",
    )(count, bra, ket, klass, factor)


STEP = 256
TILE = 160


def one_hot(index, number):
    return jnp.where(number == index.astype(jnp.int32), 1.0, 0.0).astype(jnp.bfloat16)


def quartet_kernel(
    ends_ref, blocks_ref, left_ref, right_ref, rows_ref, tables_ref,
    out_ref, scaled_ref, pieces_ref, totals_ref, found_ref, values_ref, factors_ref,
):
    classes = tables_ref.shape[0]
    pairs = pieces_ref.shape[0]
    width = totals_ref.shape[1]
    kinds = range(6)
    scaled_ref[...] = (blocks_ref[...].reshape(16, 16, SUBLANES, LANES) * left_ref[...][:, None]
                       * right_ref[...][None]).reshape(scaled_ref.shape)
    for half in range(2):
        high, low = split(scaled_ref[pl.ds(half, pairs, stride=2), :])
        pieces_ref[:, LANES * half:LANES * (half + 1)] = high
        pieces_ref[:, width + LANES * half:width + LANES * (half + 1)] = low
    totals_ref[...] = jnp.zeros_like(totals_ref)
    steps = (ends_ref[classes - 1] + STEP - 1) // STEP

    def find(index, carry):
        here = pl.ds(pl.multiple_of(index * STEP, STEP), STEP)
        columns = rows_ref[:, here].T
        number = lax.broadcasted_iota(jnp.int32, (STEP, pairs), 1)
        chosen = jnp.concatenate([one_hot(columns[:, kind:kind + 1], number) for kind in kinds], axis=0)
        found = dot(chosen, pieces_ref[...], NN).astype(jnp.bfloat16)
        for kind in kinds:
            part = slice(STEP * kind, STEP * (kind + 1))
            found_ref[kind, 0, here, :] = found[part, :width]
            found_ref[kind, 1, here, :] = found[part, width:]
            values_ref[kind, here, :] = jnp.zeros((STEP, width), jnp.float32)
        factors_ref[here, :] = jnp.broadcast_to(columns[:, 7:8], (STEP, LANES))
        return carry

    lax.fori_loop(0, steps, find, 0)

    for klass in range(classes):
        begin = 0 if klass == 0 else ends_ref[klass - 1]
        end = ends_ref[klass]
        base = begin // 16 * 16

        def multiply(index, carry):
            start = pl.multiple_of(base + index * TILE, 16)
            here = pl.ds(start, TILE)
            slot = start + lax.broadcasted_iota(jnp.int32, (TILE, width), 0)
            mine = (slot >= begin) & (slot < end)
            factor = factors_ref[here, :]
            factor = jnp.concatenate((factor, factor), axis=1)
            for kind in kinds:
                form = kind // 2
                dims = NT if kind % 2 == 0 else NN
                high, low = found_ref[kind, 0, here, :], found_ref[kind, 1, here, :]
                product = dot(jnp.concatenate((high, low), axis=0), tables_ref[klass, form, 0], dims)
                product = product[:TILE] + product[TILE:]
                product += dot(high, tables_ref[klass, form, 1], dims)
                product *= factor if kind < 2 else -0.5 * factor
                values_ref[kind, here, :] = jnp.where(mine, product, values_ref[kind, here, :])
            return carry

        lax.fori_loop(0, jnp.where(begin < end, (end - base + TILE - 1) // TILE, 0), multiply, 0)

    def add(index, carry):
        here = pl.ds(pl.multiple_of(index * STEP, STEP), STEP)
        number = lax.broadcasted_iota(jnp.int32, (pairs, STEP), 0)
        chosen = jnp.concatenate([one_hot(rows_ref[kind ^ 1:(kind ^ 1) + 1, here], number) for kind in kinds], axis=1)
        high, low = split(jnp.concatenate([values_ref[kind, here, :] for kind in kinds], axis=0))
        totals_ref[...] += dot(chosen, high, NN) + dot(chosen, low, NN)
        return carry

    lax.fori_loop(0, steps, add, 0)
    for half in range(2):
        scaled_ref[pl.ds(half, pairs, stride=2), :] = totals_ref[:, LANES * half:LANES * (half + 1)]
    out_ref[...] = (scaled_ref[...].reshape(16, 16, SUBLANES, LANES) * left_ref[...][:, None]
                    * right_ref[...][None]).reshape(out_ref.shape)


def add_quartets(ends, blocks, left, right, rows, tables):
    lines = blocks.shape[0]
    padded = rows.shape[1] + TILE
    width = tables.shape[-1]
    vmem = pl.BlockSpec(memory_space=pltpu.VMEM)
    return pl.pallas_call(
        quartet_kernel,
        out_shape=jax.ShapeDtypeStruct(blocks.shape, jnp.float32),
        in_specs=[pl.BlockSpec(memory_space=pltpu.SMEM)] + [vmem] * 5,
        out_specs=vmem,
        scratch_shapes=[
            pltpu.VMEM((lines, LANES), jnp.float32),
            pltpu.VMEM((lines // 2, 2 * width), jnp.bfloat16),
            pltpu.VMEM((lines // 2, width), jnp.float32),
            pltpu.VMEM((6, 2, padded, width), jnp.bfloat16),
            pltpu.VMEM((6, padded, width), jnp.float32),
            pltpu.VMEM((padded, LANES), jnp.float32),
        ],
        compiler_params=pltpu.CompilerParams(vmem_limit_bytes=VMEM_BYTES),
        name="add_quartets",
    )(ends, blocks, left, right, rows, tables)


def exchange(values):
    return lax.all_to_all(values, AXES, split_axis=0, concat_axis=0, tiled=True)


def on_device(
    density,
    core_hamiltonian,
    class_tables,
    shell_scale,
    block_place,
    work_blocks,
    quartet_bra,
    quartet_ket,
    quartet_class,
    quartet_factor,
    quartet_count,
):
    row_count = lax.axis_size("row")
    col_count = lax.axis_size("col")
    devices = row_count * col_count
    classes = class_tables.shape[0]
    own_tasks = work_blocks[0]
    asked = ask_blocks(work_blocks, block_place, devices)
    wanted = exchange(asked.reshape(devices, 1, LANES)).reshape(devices, LANES)
    picked, lines = pick_blocks(wanted, flatten_blocks(density))
    blocks = exchange(picked.reshape(devices, SUBLANES, LANES))
    blocks = blocks.reshape(devices * SUBLANES, LANES)

    tables = make_tables(class_tables)
    scales = shell_scale.reshape(-1, SHELL)[own_tasks]
    left = jnp.broadcast_to(
        scales.reshape(row_count, 2, 1, 2, SUBLANES, 1), (row_count, 2, 2, 2, SUBLANES, SHELL)
    ).reshape(row_count, SUBLANES, LANES)
    right = jnp.broadcast_to(
        scales.reshape(col_count, 1, 2, 1, 1, SHELL), (col_count, 2, 2, 2, SUBLANES, SHELL)
    ).reshape(col_count, SUBLANES, LANES)
    rows = sort_quartets(quartet_count, quartet_bra, quartet_ket, quartet_class, quartet_factor)
    slots = quartet_class.shape[1]
    within = jnp.where(jnp.arange(slots) < quartet_count[0], quartet_class[0], classes)
    ends = jnp.sum((within[None, :] <= jnp.arange(classes)[:, None]).astype(jnp.int32), axis=1)
    summed = add_quartets(ends, blocks, left, right, rows, tables)
    returned = exchange(summed.reshape(devices, SUBLANES, LANES))
    return merge_blocks(lines, returned.reshape(devices * SUBLANES, LANES), core_hamiltonian)


def solution(mesh):
    placed = (
        P("row", "col"),
        P("row", "col"),
        P(),
        P(),
        P(),
        P(("row", "col"), None),
        P(("row", "col"), None),
        P(("row", "col"), None),
        P(("row", "col"), None),
        P(("row", "col"), None),
        P(("row", "col")),
    )
    return jax.shard_map(
        on_device, mesh=mesh, in_specs=placed, out_specs=P("row", "col"), check_vma=False
    )
```

```python
import functools

import jax
import jax.numpy as jnp
from jax import lax
from jax.experimental import pallas as pl
from jax.experimental.pallas import tpu as pltpu
from jax.sharding import PartitionSpec as P

SHELL = 16
LANES = 128
SUBLANES = 8
STRIPE = 40
VMEM_BYTES = 24 << 20
GROUPS = LANES // SHELL
AXES = ("row", "col")
NT = (((1,), (1,)), ((), ()))
NN = (((1,), (0,)), ((), ()))


def swap_groups(tile):
    sublane = lax.broadcasted_iota(jnp.int32, tile.shape, 0)
    lane = lax.broadcasted_iota(jnp.int32, tile.shape, 1)
    group, inner = lane // SHELL, lane % SHELL
    tile = jnp.take_along_axis(tile, ((sublane + group) % GROUPS) * SHELL + inner, axis=1)
    tile = jnp.take_along_axis(tile, (sublane - group) % SUBLANES, axis=0)
    return jnp.take_along_axis(tile, ((sublane - group) % GROUPS) * SHELL + inner, axis=1)


def split(values):
    high = values.astype(jnp.bfloat16)
    low = (values - high.astype(jnp.float32)).astype(jnp.bfloat16)
    return high, low


def dot(left, right, dims):
    return lax.dot_general(left, right, dims, preferred_element_type=jnp.float32)


def ask_kernel(work_ref, place_ref, out_ref):
    tasks = work_ref.shape[1]
    devices = out_ref.shape[0]
    row = lax.broadcasted_iota(jnp.int32, (tasks, tasks), 0)
    lane = lax.broadcasted_iota(jnp.int32, (tasks, tasks), 1)
    work = jnp.sum(jnp.where(row == lane, work_ref[...], 0).astype(jnp.float32), axis=1, keepdims=True)
    work = work.astype(jnp.int32)
    lane = lax.broadcasted_iota(jnp.int32, (tasks, LANES), 1)
    table = jnp.zeros((tasks, LANES), jnp.float32)
    for part in range(place_ref.shape[0]):
        hit = work == lane + part * LANES
        table += jnp.where(hit, place_ref[part:part + 1, :], 0).astype(jnp.float32)
    place = jnp.sum(table, axis=1, keepdims=True).astype(jnp.int32) % STRIPE
    first = (place * (2 * STRIPE)).astype(jnp.float32)
    second = (place * 2).astype(jnp.float32)
    values = jnp.concatenate((first, first, second, second), axis=0)
    row = lax.broadcasted_iota(jnp.int32, (4 * tasks, LANES), 0)
    lane = lax.broadcasted_iota(jnp.int32, (4 * tasks, LANES), 1)
    values = jnp.where(lane == row // tasks, values, 0.0)
    owner = lax.broadcasted_iota(jnp.int32, (devices, 4 * tasks), 0)
    place = lax.broadcasted_iota(jnp.int32, (devices, 4 * tasks), 1)
    part, task = place // tasks, place % tasks
    index = jnp.where(part < 2, owner // (tasks // 2), owner % (tasks // 2))
    chosen = jnp.where(task == 2 * index + part % 2, 1.0, 0.0)
    asked = lax.dot_general(
        chosen, values, NN, precision=lax.Precision.HIGHEST, preferred_element_type=jnp.float32
    )
    out_ref[...] = asked.astype(jnp.int32)


def ask_blocks(work_blocks, block_place, devices):
    return pl.pallas_call(
        ask_kernel,
        out_shape=jax.ShapeDtypeStruct((devices, LANES), jnp.int32),
        compiler_params=pltpu.CompilerParams(vmem_limit_bytes=60 << 20),
        name="ask_blocks",
    )(work_blocks, block_place.reshape(-1, LANES))


def flatten_kernel(density_ref, flat_ref):
    row_blocks = density_ref.shape[0] // SHELL
    col_blocks = density_ref.shape[1] // SHELL

    def flatten(block, carry):
        for half in range(2):
            start = pl.multiple_of(block * SHELL + half * SUBLANES, SUBLANES)
            for tile in range(col_blocks // GROUPS):
                lanes = slice(tile * LANES, (tile + 1) * LANES)
                values = density_ref[pl.ds(start, SUBLANES), lanes]
                place = (block * col_blocks + tile * GROUPS) * 2 + half
                flat_ref[pl.ds(place, SUBLANES, stride=2), :] = swap_groups(values)
        return carry

    lax.fori_loop(0, row_blocks, flatten, 0, unroll=8)


def flatten_blocks(density):
    blocks = (density.shape[0] // SHELL) * (density.shape[1] // SHELL)
    return pl.pallas_call(
        flatten_kernel,
        out_shape=jax.ShapeDtypeStruct((2 * blocks, LANES), jnp.float32),
        compiler_params=pltpu.CompilerParams(vmem_limit_bytes=VMEM_BYTES),
        name="flatten_blocks",
    )(density)


def pick_kernel(wanted_ref, flat_ref, out_ref, lines_ref, turned_ref, scalars_ref, arrived):
    devices = lines_ref.shape[1]
    turned = wanted_ref[...].T
    turned_ref[...] = jnp.concatenate(
        [turned[part // 2:part // 2 + 1] + turned[2 + part % 2:3 + part % 2] for part in range(4)] * 2, axis=0
    )
    copy = pltpu.make_async_copy(turned_ref, scalars_ref, arrived)
    copy.start()
    lines_ref[...] = turned_ref[...]
    copy.wait()

    def pick(device, carry):
        for part in range(4):
            source = pl.multiple_of(scalars_ref[part, device], 2)
            target = pl.multiple_of(SUBLANES * device + 2 * part, 2)
            out_ref[pl.ds(target, 2), :] = flat_ref[pl.ds(source, 2), :]
        return carry

    lax.fori_loop(0, devices, pick, 0, unroll=8)


def pick_blocks(wanted, flat):
    devices = wanted.shape[0]
    return pl.pallas_call(
        pick_kernel,
        out_shape=(
            jax.ShapeDtypeStruct((devices * SUBLANES, LANES), jnp.float32),
            jax.ShapeDtypeStruct((SUBLANES, devices), jnp.int32),
        ),
        scratch_shapes=[
            pltpu.VMEM((SUBLANES, devices), jnp.int32),
            pltpu.SMEM((SUBLANES, devices), jnp.int32),
            pltpu.SemaphoreType.DMA,
        ],
        compiler_params=pltpu.CompilerParams(vmem_limit_bytes=VMEM_BYTES),
        name="pick_blocks",
    )(wanted, flat)


def merge_kernel(wanted_ref, parts_ref, core_ref, out_ref, flat_ref, other_ref, near_ref, sent):
    row_blocks = core_ref.shape[0] // SHELL
    col_blocks = core_ref.shape[1] // SHELL
    devices = parts_ref.shape[0] // SUBLANES
    flat_ref[...] = jnp.zeros_like(flat_ref)
    other_ref[...] = jnp.zeros_like(other_ref)

    def add(pair, carry):
        todo = []
        for which, ref in enumerate((flat_ref, other_ref)):
            device = 2 * pair + which
            for part in range(4):
                place = pl.ds(pl.multiple_of(wanted_ref[part, device], 2), 2)
                source = pl.multiple_of(SUBLANES * device + 2 * part, 2)
                todo.append((ref, place, ref[place, :] + parts_ref[pl.ds(source, 2), :]))
        for ref, place, value in todo:
            ref[place, :] = value
        return carry

    lax.fori_loop(0, devices // 2, add, 0, unroll=8)

    def unflatten(block, carry):
        for half in range(2):
            start = pl.multiple_of(block * SHELL + half * SUBLANES, SUBLANES)
            for tile in range(col_blocks // GROUPS):
                lanes = slice(tile * LANES, (tile + 1) * LANES)
                place = (block * col_blocks + tile * GROUPS) * 2 + half
                spread = pl.ds(place, SUBLANES, stride=2)
                values = swap_groups(flat_ref[spread, :] + other_ref[spread, :])
                near_ref[pl.ds(start, SUBLANES), lanes] = core_ref[pl.ds(start, SUBLANES), lanes] + values
        return carry

    copies = []
    for chunk in range(row_blocks // GROUPS):
        lax.fori_loop(chunk * GROUPS, (chunk + 1) * GROUPS, unflatten, 0, unroll=GROUPS)
        rows = pl.ds(chunk * LANES, LANES)
        copies.append(pltpu.make_async_copy(near_ref.at[rows], out_ref.at[rows], sent.at[chunk]))
        copies[-1].start()
    for copy in copies:
        copy.wait()


def merge_blocks(wanted, parts, core):
    blocks = (core.shape[0] // SHELL) * (core.shape[1] // SHELL)
    return pl.pallas_call(
        merge_kernel,
        out_shape=jax.ShapeDtypeStruct(core.shape, jnp.float32),
        in_specs=[
            pl.BlockSpec(memory_space=pltpu.SMEM),
            pl.BlockSpec(memory_space=pltpu.VMEM),
            pl.BlockSpec(memory_space=pltpu.VMEM),
        ],
        out_specs=pl.BlockSpec(memory_space=pl.ANY),
        scratch_shapes=[
            pltpu.VMEM((2 * blocks, LANES), jnp.float32),
            pltpu.VMEM((2 * blocks, LANES), jnp.float32),
            pltpu.VMEM(core.shape, jnp.float32),
            pltpu.SemaphoreType.DMA((core.shape[0] // LANES,)),
        ],
        compiler_params=pltpu.CompilerParams(vmem_limit_bytes=VMEM_BYTES),
        name="merge_blocks",
    )(wanted, parts, core)


def table_kernel(tables_ref, out_ref, mid_ref, turned_ref, last_ref):
    width = tables_ref.shape[1]
    halves = range(2)

    def keep(form, values):
        out_ref[0, form, 0], out_ref[0, form, 1] = split(values)

    keep(0, tables_ref[0])

    def swap_inner(first, carry):
        for a in halves:
            for b in halves:
                rows = pl.ds(pl.multiple_of(first * SHELL + SUBLANES * a, SUBLANES), SUBLANES)
                values = tables_ref[0, rows, LANES * b:LANES * (b + 1)]
                rows = pl.ds(pl.multiple_of(first * SHELL + SUBLANES * b, SUBLANES), SUBLANES)
                mid_ref[rows, LANES * a:LANES * (a + 1)] = swap_groups(values)
        return carry

    lax.fori_loop(0, width // SHELL, swap_inner, 0, unroll=4)
    turned = mid_ref[...].T
    keep(1, mid_ref[...])
    for b in halves:
        turned_ref[b] = turned[:, LANES * b:LANES * (b + 1)]

    def swap_outer(last, carry):
        for a in halves:
            for b in halves:
                rows = pl.ds(LANES * a + last, SUBLANES, stride=SHELL)
                values = turned_ref[b, rows, :]
                rows = pl.ds(LANES * b + last, SUBLANES, stride=SHELL)
                last_ref[a, rows, :] = swap_groups(values)
        return carry

    lax.fori_loop(0, SHELL, swap_outer, 0, unroll=4)
    last = jnp.concatenate((last_ref[0], last_ref[1]), axis=1)
    keep(2, last)


def make_tables(class_tables):
    classes, width, _ = class_tables.shape
    return pl.pallas_call(
        table_kernel,
        grid=(classes,),
        out_shape=jax.ShapeDtypeStruct((classes, 3, 2, width, width), jnp.bfloat16),
        in_specs=[pl.BlockSpec((1, width, width), lambda c: (c, 0, 0))],
        out_specs=pl.BlockSpec((1, 3, 2, width, width), lambda c: (c, 0, 0, 0, 0)),
        scratch_shapes=[
            pltpu.VMEM((width, width), jnp.float32),
            pltpu.VMEM((2, width, LANES), jnp.float32),
            pltpu.VMEM((2, width, LANES), jnp.float32),
        ],
        compiler_params=pltpu.CompilerParams(vmem_limit_bytes=VMEM_BYTES),
        name="make_tables",
    )(class_tables)


def sort_kernel(count_ref, bra_ref, ket_ref, class_ref, factor_ref, rows_ref):
    slots = bra_ref.shape[1]
    bra, ket = bra_ref[...], ket_ref[...]
    shell_a, shell_b = bra // 32, bra % 32
    shell_c, shell_d = ket // 32, ket % 32
    slot = lax.broadcasted_iota(jnp.int32, (1, slots), 1)
    live = slot < count_ref[0]
    klass = jnp.where(live, class_ref[...], SUBLANES - 1)
    factor = jnp.where(live, factor_ref[...], 0.0)

    def line(first, second):
        return (((first // 2) * 16 + second // 2) * 4 + (first % 2) * 2 + second % 2).astype(jnp.float32)

    fields = jnp.concatenate(
        (
            line(shell_c, shell_d),
            line(shell_a, shell_b),
            line(shell_b, shell_d),
            line(shell_a, shell_c),
            line(shell_b, shell_c),
            line(shell_a, shell_d),
            klass.astype(jnp.float32),
            factor,
        ),
        axis=0,
    )
    number = lax.broadcasted_iota(jnp.int32, (SUBLANES, slots), 0)
    same = jnp.where(klass == number, 1.0, 0.0)
    start = jnp.sum(jnp.where(klass < number, 1.0, 0.0), axis=1, keepdims=True)
    low = lax.broadcasted_iota(jnp.int32, (slots, slots), 0)
    high = lax.broadcasted_iota(jnp.int32, (slots, slots), 1)
    before = jnp.where(low < high, 1.0, 0.0).astype(jnp.bfloat16)
    rank = dot(same.astype(jnp.bfloat16), before, NN) + start
    rank = jnp.sum(rank * same, axis=0, keepdims=True).astype(jnp.int32)
    order = jnp.where(low == rank, 1.0, 0.0)
    rows_ref[...] = lax.dot_general(
        fields, order, NT, precision=lax.Precision.HIGHEST, preferred_element_type=jnp.float32
    )


def sort_quartets(count, bra, ket, klass, factor):
    slots = bra.shape[1]
    vmem = pl.BlockSpec(memory_space=pltpu.VMEM)
    return pl.pallas_call(
        sort_kernel,
        out_shape=jax.ShapeDtypeStruct((SUBLANES, slots), jnp.float32),
        in_specs=[pl.BlockSpec(memory_space=pltpu.SMEM)] + [vmem] * 4,
        out_specs=vmem,
        compiler_params=pltpu.CompilerParams(vmem_limit_bytes=VMEM_BYTES),
        name="sort_quartets",
    )(count, bra, ket, klass, factor)


STEP = 256
TILE = 160


def one_hot(index, number):
    return jnp.where(number == index.astype(jnp.int32), 1.0, 0.0).astype(jnp.bfloat16)


def quartet_kernel(
    ends_ref, blocks_ref, left_ref, right_ref, rows_ref, tables_ref,
    out_ref, scaled_ref, pieces_ref, totals_ref, found_ref, values_ref, factors_ref,
):
    classes = tables_ref.shape[0]
    pairs = pieces_ref.shape[0]
    width = totals_ref.shape[1]
    kinds = range(6)
    scaled_ref[...] = (blocks_ref[...].reshape(16, 16, SUBLANES, LANES) * left_ref[...][:, None]
                       * right_ref[...][None]).reshape(scaled_ref.shape)
    for half in range(2):
        high, low = split(scaled_ref[pl.ds(half, pairs, stride=2), :])
        pieces_ref[:, LANES * half:LANES * (half + 1)] = high
        pieces_ref[:, width + LANES * half:width + LANES * (half + 1)] = low
    totals_ref[...] = jnp.zeros_like(totals_ref)
    steps = (ends_ref[classes - 1] + STEP - 1) // STEP

    def find(index, carry):
        here = pl.ds(pl.multiple_of(index * STEP, STEP), STEP)
        columns = rows_ref[:, here].T
        number = lax.broadcasted_iota(jnp.int32, (STEP, pairs), 1)
        chosen = jnp.concatenate([one_hot(columns[:, kind:kind + 1], number) for kind in kinds], axis=0)
        found = dot(chosen, pieces_ref[...], NN).astype(jnp.bfloat16)
        for kind in kinds:
            part = slice(STEP * kind, STEP * (kind + 1))
            found_ref[kind, 0, here, :] = found[part, :width]
            found_ref[kind, 1, here, :] = found[part, width:]
            values_ref[kind, here, :] = jnp.zeros((STEP, width), jnp.float32)
        factors_ref[here, :] = jnp.broadcast_to(columns[:, 7:8], (STEP, LANES))
        return carry

    lax.fori_loop(0, steps, find, 0)

    for klass in range(classes):
        begin = 0 if klass == 0 else ends_ref[klass - 1]
        end = ends_ref[klass]
        base = begin // 16 * 16

        def multiply(index, carry):
            start = pl.multiple_of(base + index * TILE, 16)
            here = pl.ds(start, TILE)
            slot = start + lax.broadcasted_iota(jnp.int32, (TILE, width), 0)
            mine = (slot >= begin) & (slot < end)
            factor = factors_ref[here, :]
            factor = jnp.concatenate((factor, factor), axis=1)
            for kind in kinds:
                form = kind // 2
                dims = NT if kind % 2 == 0 else NN
                high, low = found_ref[kind, 0, here, :], found_ref[kind, 1, here, :]
                product = dot(jnp.concatenate((high, low), axis=0), tables_ref[klass, form, 0], dims)
                product = product[:TILE] + product[TILE:]
                product += dot(high, tables_ref[klass, form, 1], dims)
                product *= factor if kind < 2 else -0.5 * factor
                values_ref[kind, here, :] = jnp.where(mine, product, values_ref[kind, here, :])
            return carry

        lax.fori_loop(0, jnp.where(begin < end, (end - base + TILE - 1) // TILE, 0), multiply, 0)

    def add(index, carry):
        here = pl.ds(pl.multiple_of(index * STEP, STEP), STEP)
        number = lax.broadcasted_iota(jnp.int32, (pairs, STEP), 0)
        chosen = jnp.concatenate([one_hot(rows_ref[kind ^ 1:(kind ^ 1) + 1, here], number) for kind in kinds], axis=1)
        high, low = split(jnp.concatenate([values_ref[kind, here, :] for kind in kinds], axis=0))
        totals_ref[...] += dot(chosen, high, NN) + dot(chosen, low, NN)
        return carry

    lax.fori_loop(0, steps, add, 0)
    for half in range(2):
        scaled_ref[pl.ds(half, pairs, stride=2), :] = totals_ref[:, LANES * half:LANES * (half + 1)]
    out_ref[...] = (scaled_ref[...].reshape(16, 16, SUBLANES, LANES) * left_ref[...][:, None]
                    * right_ref[...][None]).reshape(out_ref.shape)


def add_quartets(ends, blocks, left, right, rows, tables):
    lines = blocks.shape[0]
    padded = rows.shape[1] + TILE
    width = tables.shape[-1]
    vmem = pl.BlockSpec(memory_space=pltpu.VMEM)
    return pl.pallas_call(
        quartet_kernel,
        out_shape=jax.ShapeDtypeStruct(blocks.shape, jnp.float32),
        in_specs=[pl.BlockSpec(memory_space=pltpu.SMEM)] + [vmem] * 5,
        out_specs=vmem,
        scratch_shapes=[
            pltpu.VMEM((lines, LANES), jnp.float32),
            pltpu.VMEM((lines // 2, 2 * width), jnp.bfloat16),
            pltpu.VMEM((lines // 2, width), jnp.float32),
            pltpu.VMEM((6, 2, padded, width), jnp.bfloat16),
            pltpu.VMEM((6, padded, width), jnp.float32),
            pltpu.VMEM((padded, LANES), jnp.float32),
        ],
        compiler_params=pltpu.CompilerParams(vmem_limit_bytes=VMEM_BYTES),
        name="add_quartets",
    )(ends, blocks, left, right, rows, tables)


def exchange(values):
    return lax.all_to_all(values, AXES, split_axis=0, concat_axis=0, tiled=True)


def on_device(
    density,
    core_hamiltonian,
    class_tables,
    shell_scale,
    block_place,
    work_blocks,
    quartet_bra,
    quartet_ket,
    quartet_class,
    quartet_factor,
    quartet_count,
):
    row_count = lax.axis_size("row")
    col_count = lax.axis_size("col")
    devices = row_count * col_count
    classes = class_tables.shape[0]
    own_tasks = work_blocks[0]
    asked = ask_blocks(work_blocks, block_place, devices)
    wanted = exchange(asked.reshape(devices, 1, LANES)).reshape(devices, LANES)
    picked, lines = pick_blocks(wanted, flatten_blocks(density))
    blocks = exchange(picked.reshape(devices, SUBLANES, LANES))
    blocks = blocks.reshape(devices * SUBLANES, LANES)

    tables = make_tables(class_tables)
    scales = shell_scale.reshape(-1, SHELL)[own_tasks]
    left = jnp.broadcast_to(
        scales.reshape(row_count, 2, 1, 2, SUBLANES, 1), (row_count, 2, 2, 2, SUBLANES, SHELL)
    ).reshape(row_count, SUBLANES, LANES)
    right = jnp.broadcast_to(
        scales.reshape(col_count, 1, 2, 1, 1, SHELL), (col_count, 2, 2, 2, SUBLANES, SHELL)
    ).reshape(col_count, SUBLANES, LANES)
    rows = sort_quartets(quartet_count, quartet_bra, quartet_ket, quartet_class, quartet_factor)
    slots = quartet_class.shape[1]
    within = jnp.where(jnp.arange(slots) < quartet_count[0], quartet_class[0], classes)
    ends = jnp.sum((within[None, :] <= jnp.arange(classes)[:, None]).astype(jnp.int32), axis=1)
    summed = add_quartets(ends, blocks, left, right, rows, tables)
    returned = exchange(summed.reshape(devices, SUBLANES, LANES))
    return merge_blocks(lines, returned.reshape(devices * SUBLANES, LANES), core_hamiltonian)


def solution(mesh):
    placed = (
        P("row", "col"),
        P("row", "col"),
        P(),
        P(),
        P(),
        P(("row", "col"), None),
        P(("row", "col"), None),
        P(("row", "col"), None),
        P(("row", "col"), None),
        P(("row", "col"), None),
        P(("row", "col")),
    )
    return jax.shard_map(
        on_device, mesh=mesh, in_specs=placed, out_specs=P("row", "col"), check_vma=False
    )
```
